512 devices in a mesh: occ: 8 (over x, core), aux: 16 (over y_lo, z), vir: 4 (over y_hi).
Axes of the slice: x: 4, y: 8 (y_hi: 4, y_lo: 2; y = y_hi * 2 + y_lo), z: 8, core: 2. Of those that a mesh axis runs over, the one named last changes fastest.
Arguments:
- bq: float32 [8, 10112, 3072], P('occ', 'aux', 'vir'), may hold values from -1.5 to 1.5
- eps_occ: float32 [8], replicated, may hold values from -1.5 to -0.3
- eps_vir: float32 [3072], P('vir'), may hold values from 0.2 to 3
- tile_pairs: int32 [8, 8, 4, 2], P('occ', None, 'vir'), may hold values from 0 to 35, as said below
- live_counts: int32 [8, 8], P('occ'), may hold values from 1 to 2, as said below
Outputs:
- gamma: float32 [8, 10112, 3072], P('occ', 'aux', 'vir')
- pair_energy: float32 [8, 8], P('occ')
The draws below stay inside these ranges and needn't reach their ends.
Inputs may be any that keep to these rules, and one draw needn't show every extreme that they name: `tile_pairs`: the 2 entries of one list are distinct. `live_counts`: every occupied orbital i has some j with all 2 slots live.
All inputs are finite; a program needn't handle non-finite values.
Results may differ from the reference program's by a relative error of at most 0.0003.
Values sent between devices are 32-bit elements; how exact they have to be, the bound alone decides.
No kernel may reach another device: no remote copies, remote signals or barrier semaphores. Data moves between devices by JAX's collectives and lax.ppermute only.
A program may use at most 64 MiB of HBM per device.

```python
import jax
import jax.numpy as jnp
from jax import lax

NAUX = 10112
NVIR = 3072
TILE = 128
KEEP = 2
NOCC = 8
N_VIR = 4


def shuffled_row(row_key):
    tile_count = NVIR // N_VIR // TILE
    return jax.random.permutation(row_key, tile_count * tile_count)


def draw_tile_pairs(key, part):
    key = jax.random.fold_in(key, 11)
    row_keys = jax.random.split(key, NOCC * NOCC * N_VIR)
    orders = jax.vmap(shuffled_row)(row_keys)
    return orders[:, :KEEP].astype(jnp.int32).reshape(NOCC, NOCC, N_VIR, KEEP)


def draw_live_counts(key, part):
    key = jax.random.fold_in(key, 23)
    first_key, second_key = jax.random.split(key)
    counts = jax.random.randint(first_key, (NOCC, NOCC), 1, KEEP + 1)
    offset = jax.random.randint(second_key, (), 0, NOCC)
    row_index = jnp.arange(NOCC)[:, None]
    col_index = jnp.arange(NOCC)[None, :]
    full_pair = col_index == (row_index + offset) % NOCC
    return jnp.where(full_pair, KEEP, counts).astype(jnp.int32)


def steps_of(own_key, shape, cuts, least, top_value):
    gain, own = 1.0, jax.random.fold_in(own_key, 6)
    for axis_at, blocks in cuts:
        draws = jnp.exp(jax.random.uniform(jax.random.fold_in(own, axis_at), (blocks,), jnp.float32, least / len(cuts), top_value / len(cuts)))
        gain = gain * jnp.repeat(draws, shape[axis_at] // blocks).reshape([-1 if axis == axis_at else 1 for axis in range(len(shape))])
    return gain


def gaussian(stream_key, extent, width, limit, shards=(), kind=jnp.bfloat16):
    entries = jax.random.normal(stream_key, extent, jnp.float32) * width
    if len(shards) > 0:
        entries = steps_of(stream_key, extent, shards, -0.22, 0.18) * entries
    return jnp.clip(entries, min=-limit, max=limit).astype(kind)


def setup_inputs(seed: int = 0) -> dict:
    splits = jax.random.split(jax.random.key(seed), 6)
    bq = gaussian(splits[0], (NOCC, NAUX, NVIR), 0.1, 1.5, ((0, 8), (1, 16), (2, 4)), jnp.float32)
    eps_occ = jnp.clip(jax.random.uniform(splits[1], (NOCC,), jnp.float32, -1.5, -0.3), -1.5, -0.3)
    eps_vir = jnp.clip(0.2 + 2.8 * jax.random.uniform(splits[2], (NVIR,), jnp.float32) ** steps_of(splits[2], (NVIR,), ((0, 4),), -0.2, 0.2), 0.2, 3.0)
    tile_pairs = draw_tile_pairs(jax.random.fold_in(splits[5], 71), 0)
    live_counts = draw_live_counts(jax.random.fold_in(splits[5], 71), 0)
    return {"bq": bq, "eps_occ": eps_occ, "eps_vir": eps_vir, "tile_pairs": tile_pairs, "live_counts": live_counts}


def reference(bq, eps_occ, eps_vir, tile_pairs, live_counts):
    tile_count = NVIR // N_VIR // TILE
    blocks = bq.reshape(NOCC, NAUX, N_VIR, tile_count, TILE)
    vir_levels = eps_vir.reshape(N_VIR, tile_count, TILE)
    slot_index = jnp.arange(KEEP).astype(jnp.int32)
    tile_index = jnp.arange(tile_count).astype(jnp.int32)
    highest = lax.Precision.HIGHEST

    def per_orbital(orbital):
        left_all = blocks[orbital]

        def per_partner(gamma_sum, partner):
            right_all = blocks[partner]
            chosen = tile_pairs[orbital, partner]
            first_tile = chosen // tile_count
            second_tile = chosen % tile_count
            left_cols = jnp.take_along_axis(left_all, first_tile[None, :, :, None], axis=2)
            right_cols = jnp.take_along_axis(right_all, second_tile[None, :, :, None], axis=2)
            coulomb = jnp.einsum('pvkx,pvky->vkxy', left_cols, right_cols, precision=highest)
            vir_first = jnp.take_along_axis(vir_levels, first_tile[:, :, None], axis=1)
            vir_second = jnp.take_along_axis(vir_levels, second_tile[:, :, None], axis=1)
            denominator = eps_occ[orbital] + eps_occ[partner] - vir_first[:, :, :, None] - vir_second[:, :, None, :]
            live_slots = (slot_index < live_counts[orbital, partner]).astype(jnp.float32)
            amplitude = coulomb / denominator * live_slots[None, :, None, None]
            contribution = jnp.einsum('vkxy,pvky->pvkx', amplitude, right_cols, precision=highest)
            onehot = (first_tile[:, :, None] == tile_index[None, None, :]).astype(jnp.float32)
            gamma_sum = gamma_sum + jnp.einsum('pvkx,vkt->pvtx', contribution, onehot, precision=highest)
            return gamma_sum, jnp.sum(coulomb * amplitude)

        start = jnp.zeros((NAUX, N_VIR, tile_count, TILE), jnp.float32)
        gamma_sum, energy_row = lax.scan(per_partner, start, jnp.arange(NOCC).astype(jnp.int32))
        return gamma_sum.reshape(NAUX, NVIR), energy_row

    gamma, pair_energy = lax.map(per_orbital, jnp.arange(NOCC).astype(jnp.int32))
    return gamma, pair_energy
```

```python
import functools

import jax
import jax.numpy as jnp
from jax import lax
from jax.experimental import pallas as pl
from jax.experimental.pallas import tpu as pltpu
from jax.sharding import PartitionSpec as P

TILE = 128
VMEM = pl.BlockSpec(memory_space=pltpu.VMEM)
SMEM = pl.BlockSpec(memory_space=pltpu.SMEM)
GROUPS = (
    ((0, 0), (0, 1), (1, 0), (3, 0)),
    ((1, 1), (3, 1), (2, 0), (2, 1)),
)


def params():
    return pltpu.CompilerParams(vmem_limit_bytes=48 * 1024 * 1024)


def cost(flops, moved):
    return pl.CostEstimate(flops=flops, bytes_accessed=moved, transcendentals=0)


def split(value):
    high = value.astype(jnp.bfloat16)
    low = (value - high.astype(jnp.float32)).astype(jnp.bfloat16)
    return high, low


def lanes(index):
    return pl.ds(pl.multiple_of(index * TILE, TILE), TILE)


def pick_kernel(index_ref, block_ref, *out_refs):
    rows = block_ref.shape[0]
    for k, out_ref in enumerate(out_refs):
        for s in range(2):
            out_ref[:rows, s * TILE : (s + 1) * TILE] = block_ref[:, lanes(index_ref[2 * k + s])]
        out_ref[rows:, :] = jnp.zeros((out_ref.shape[0] - rows, 2 * TILE), jnp.float32)


def pick(index, block, count, padded):
    return pl.pallas_call(
        pick_kernel,
        out_shape=[jax.ShapeDtypeStruct((padded, 2 * TILE), jnp.float32)] * count,
        in_specs=[SMEM, VMEM],
        out_specs=[VMEM] * count,
        compiler_params=params(),
        cost_estimate=cost(0, count * padded * 4 * TILE * 4),
        name="pick",
    )(index, block)


def left_kernel(block_ref, out_ref):
    rows = block_ref.shape[0]
    padded = out_ref.shape[2]
    for f in range(out_ref.shape[0]):
        tile = block_ref[:, f * TILE : (f + 1) * TILE]
        tile = jnp.concatenate([tile, jnp.zeros((padded - rows, TILE), jnp.float32)], axis=0)
        high, low = split(tile.T)
        out_ref[f, :TILE, :] = high
        out_ref[f, TILE:, :] = low


def left(block, padded):
    tiles = block.shape[1] // TILE
    return pl.pallas_call(
        left_kernel,
        out_shape=jax.ShapeDtypeStruct((tiles, 2 * TILE, padded), jnp.bfloat16),
        in_specs=[VMEM],
        out_specs=VMEM,
        compiler_params=params(),
        cost_estimate=cost(0, block.size * 8),
        name="left",
    )(block)


def coulomb_kernel(first_ref, left_ref, *refs):
    out_ref = refs[-1]
    for k, right_ref in enumerate(refs[:-1]):
        for s in range(2):
            t = 2 * k + s
            high, low = split(right_ref[:, s * TILE : (s + 1) * TILE])
            both = jnp.concatenate([high, low], axis=1)
            part = jnp.dot(left_ref[first_ref[t]], both, preferred_element_type=jnp.float32)
            cross = part[:TILE, TILE:] + part[TILE:, :TILE] + part[TILE:, TILE:]
            total = part[:TILE, :TILE] + cross
            out_ref[:, 8 * t : 8 * t + 8, :] = total.reshape(TILE // 8, 8, TILE)


def coulomb(first, left_split, rights):
    count = 2 * len(rights)
    padded = rights[0].shape[0]
    return pl.pallas_call(
        coulomb_kernel,
        out_shape=jax.ShapeDtypeStruct((TILE // 8, 8 * count, TILE), jnp.float32),
        in_specs=[SMEM, VMEM] + [VMEM] * len(rights),
        out_specs=VMEM,
        compiler_params=params(),
        cost_estimate=cost(count * 8 * TILE * TILE * padded, count * padded * TILE * 8),
        name="coulomb",
    )(first, left_split, *rights)


def amplitude_kernel(parts_ref, denominator_ref, out_ref):
    summed = jnp.sum(parts_ref[...], axis=0)
    amplitude = summed / denominator_ref[...]
    tiles = summed.shape[0] // 8
    energy = jnp.sum((summed * amplitude).reshape(tiles, 8, TILE), axis=1)
    extra = out_ref.shape[1] - summed.shape[0]
    energy = jnp.concatenate([energy, jnp.zeros((extra - tiles, TILE), jnp.float32)], axis=0) if extra > tiles else energy
    for owner in range(out_ref.shape[0]):
        out_ref[owner, : 8 * tiles, :] = amplitude
        out_ref[owner, 8 * tiles :, :] = energy


def amplitude(parts, denominator):
    owners, rows, _ = parts.shape
    extra = -(-(rows // 8) // 8) * 8
    return pl.pallas_call(
        amplitude_kernel,
        out_shape=jax.ShapeDtypeStruct((owners, rows + extra, TILE), jnp.float32),
        in_specs=[VMEM, VMEM],
        out_specs=VMEM,
        compiler_params=params(),
        cost_estimate=cost(owners * rows * TILE, 2 * owners * rows * TILE * 4),
        name="amplitude",
    )(parts, denominator)


def gamma_kernel(carried, first_ref, amplitude_ref, *refs):
    if carried:
        gamma_in, *refs = refs
    *right_refs, gamma_ref, energy_ref = refs
    rows = gamma_ref.shape[0]
    count = 2 * len(right_refs)
    gamma_ref[...] = gamma_in[...] if carried else jnp.zeros_like(gamma_ref)
    for k, right_ref in enumerate(right_refs):
        for s in range(2):
            t = 2 * k + s
            value = amplitude_ref[:, 8 * t : 8 * t + 8, :].reshape(TILE, TILE)
            high, low = split(value)
            weights = jnp.concatenate(
                [
                    jnp.concatenate([high, high], axis=1),
                    jnp.concatenate([low, low], axis=1),
                ],
                axis=0,
            )
            both = jnp.concatenate(split(right_ref[:, s * TILE : (s + 1) * TILE]), axis=1)
            part = lax.dot_general(both, weights, (((1,), (1,)), ((), ())), preferred_element_type=jnp.float32)
            place = lanes(first_ref[t])
            gamma_ref[:, place] += (part[:, :TILE] + part[:, TILE:])[:rows]
    energy_ref[...] = jnp.sum(amplitude_ref[:, 8 * count :, :], axis=0)


def gamma_add(first, amplitudes, rights, rows, cols, carried):
    count = 2 * len(rights)
    padded = rights[0].shape[0]
    extra = amplitudes.shape[1] - 8 * count
    inputs = (first, amplitudes) + ((carried,) if carried is not None else ())
    return pl.pallas_call(
        functools.partial(gamma_kernel, carried is not None),
        out_shape=[
            jax.ShapeDtypeStruct((rows, cols), jnp.float32),
            jax.ShapeDtypeStruct((extra, TILE), jnp.float32),
        ],
        in_specs=[SMEM] + [VMEM] * (len(inputs) - 1 + len(rights)),
        out_specs=[VMEM, VMEM],
        compiler_params=params(),
        cost_estimate=cost(count * 8 * TILE * TILE * padded, count * padded * TILE * 8),
        name="gamma",
    )(*inputs, *rights)


def per_device(bq, eps_occ, eps_vir, tile_pairs, live_counts):
    occ_size = lax.axis_size("occ")
    me = lax.axis_index("occ")
    chip, core = me // 2, me % 2
    chips = occ_size // 2
    owner = lax.axis_index("aux")
    block = bq[0]
    rows, cols = block.shape
    padded = -(-rows // 16) * 16
    tile_count = cols // TILE
    own_pairs = tile_pairs[0, :, 0, :]
    all_pairs = lax.all_gather(own_pairs, "occ")

    shifts = [shift for group in GROUPS for shift in group]
    receivers = jnp.stack([(chip + dx) % chips * 2 + (core + dc) % 2 for dx, dc in shifts])
    partners = jnp.stack([(chip - dx) % chips * 2 + (core - dc) % 2 for dx, dc in shifts])
    wanted = all_pairs[receivers, me] % tile_count
    chosen = own_pairs[partners]
    first = (chosen // tile_count).astype(jnp.int32)
    second = chosen % tile_count

    left_split = left(block, padded)
    picked = pick(wanted.reshape(-1), block, len(shifts), padded)
    held = {}
    for shift, tiles in zip(shifts, picked):
        dx, dc = shift
        if shift == (0, 0):
            held[shift] = tiles
        else:
            route = [(x * 2 + c, (x + dx) % chips * 2 + (c + dc) % 2) for x in range(chips) for c in range(2)]
            held[shift] = lax.ppermute(tiles, "occ", route)

    vir_rows = eps_vir.reshape(tile_count, TILE // 8, 8)[:, owner]
    vir_tiles = eps_vir.reshape(tile_count, TILE)
    pair_level = eps_occ[me] + eps_occ[partners]
    denominator = pair_level[:, None, None, None] - vir_rows[first][:, :, :, None] - vir_tiles[second][:, :, None, :]
    live = jnp.arange(2)[None, :] < live_counts[0][partners][:, None]
    denominator = jnp.where(live[:, :, None, None], denominator, jnp.inf)

    total, energies, at = None, [], 0
    for group in GROUPS:
        here = slice(at, at + len(group))
        at += len(group)
        rights = [held[shift] for shift in group]
        place = first[here].reshape(-1)
        parts = coulomb(place, left_split, rights)
        parts = lax.all_to_all(parts, "aux", 0, 0)
        amplitudes = amplitude(parts, denominator[here].reshape(-1, TILE))
        amplitudes = lax.all_to_all(amplitudes, "aux", 0, 0)
        total, energy = gamma_add(place, amplitudes, rights, rows, cols, total)
        energies.append(jnp.sum(energy[: 2 * len(group)].reshape(len(group), 2 * TILE), axis=1))
    energy = jnp.concatenate(energies)
    mine = partners[:, None] == jnp.arange(occ_size)[None, :]
    energy = jnp.sum(jnp.where(mine, energy[:, None], 0.0), axis=0)
    energy = lax.psum(energy[None], "vir")
    return total[None], energy


def solution(mesh):
    return jax.shard_map(
        per_device,
        mesh=mesh,
        in_specs=(
            P("occ", "aux", "vir"),
            P(),
            P("vir"),
            P("occ", None, "vir", None),
            P("occ", None),
        ),
        out_specs=(P("occ", "aux", "vir"), P("occ", None)),
        check_vma=False,
    )
```

```python
import functools

import jax
import jax.numpy as jnp
from jax import lax
from jax.experimental import pallas as pl
from jax.experimental.pallas import tpu as pltpu
from jax.sharding import PartitionSpec as P

TILE = 128
VMEM = pl.BlockSpec(memory_space=pltpu.VMEM)
SMEM = pl.BlockSpec(memory_space=pltpu.SMEM)
def params():
    return pltpu.CompilerParams(vmem_limit_bytes=12 * 1024 * 1024)


def cost(flops, moved):
    return pl.CostEstimate(flops=flops, bytes_accessed=moved, transcendentals=0)


def split(value):
    high = value.astype(jnp.bfloat16)
    low = (value - high.astype(jnp.float32)).astype(jnp.bfloat16)
    return high, low


def lanes(index):
    return pl.ds(pl.multiple_of(index * TILE, TILE), TILE)


def pick_kernel(index_ref, block_ref, *out_refs):
    rows = block_ref.shape[0]
    at = 0
    for out_ref in out_refs:
        for k in range(out_ref.shape[0]):
            for s in range(2):
                out_ref[k, :rows, s * TILE : (s + 1) * TILE] = block_ref[:, lanes(index_ref[at])]
                at += 1
            out_ref[k, rows:, :] = jnp.zeros((out_ref.shape[1] - rows, 2 * TILE), jnp.float32)


def pick(wanted, block, counts, padded):
    return pl.pallas_call(
        pick_kernel,
        out_shape=[jax.ShapeDtypeStruct((count, padded, 2 * TILE), jnp.float32) for count in counts],
        in_specs=[SMEM, VMEM],
        out_specs=[VMEM] * len(counts),
        compiler_params=params(),
        cost_estimate=cost(0, sum(counts) * padded * 4 * TILE * 4),
        name="pick",
    )(wanted, block)


def left_kernel(block_ref, out_ref):
    rows = block_ref.shape[0]
    padded = out_ref.shape[2]
    for f in range(out_ref.shape[0]):
        tile = block_ref[:, f * TILE : (f + 1) * TILE]
        tile = jnp.concatenate([tile, jnp.zeros((padded - rows, TILE), jnp.float32)], axis=0)
        high, low = split(tile.T)
        out_ref[f, :TILE, :] = high
        out_ref[f, TILE:, :] = low


def left(block, padded):
    tiles = block.shape[1] // TILE
    return pl.pallas_call(
        left_kernel,
        out_shape=jax.ShapeDtypeStruct((tiles, 2 * TILE, padded), jnp.bfloat16),
        in_specs=[VMEM],
        out_specs=VMEM,
        compiler_params=params(),
        cost_estimate=cost(0, block.size * 8),
        name="left",
    )(block)


def add_amplitude(parts_ref, denominator_ref, out_ref):
    summed = jnp.sum(parts_ref[...], axis=0)
    amplitude = summed / denominator_ref[...]
    tiles = summed.shape[0] // 8
    energy = jnp.sum((summed * amplitude).reshape(tiles, 8, TILE), axis=1)
    energy = jnp.concatenate([energy, jnp.zeros((-tiles % 8, TILE), jnp.float32)], axis=0) if tiles % 8 else energy
    done = 8 * tiles + energy.shape[0]
    for owner in range(out_ref.shape[0]):
        out_ref[owner, : 8 * tiles, :] = amplitude
        out_ref[owner, 8 * tiles : done, :] = energy
    return done


def returned_rows(tiles):
    return 8 * tiles + -(-tiles // 8) * 8


def exchange_kernel(entries, with_parts, *refs):
    *in_refs, out_ref = refs
    at = 0
    if with_parts:
        parts_ref, denominator_ref, *in_refs = in_refs
        at = add_amplitude(parts_ref, denominator_ref, out_ref)
    if entries:
        first_ref, left_ref, *right_refs = in_refs
        for k, (which, entry) in enumerate(entries):
            for s in range(2):
                t = 2 * k + s
                high, low = split(right_refs[which][entry, :, s * TILE : (s + 1) * TILE])
                both = jnp.concatenate([high, low], axis=1)
                part = jnp.dot(left_ref[first_ref[t]], both, preferred_element_type=jnp.float32)
                cross = part[:TILE, TILE:] + part[TILE:, :TILE] + part[TILE:, TILE:]
                total = part[:TILE, :TILE] + cross
                out_ref[:, at + 8 * t : at + 8 * t + 8, :] = total.reshape(TILE // 8, 8, TILE)


def exchange(returned, group):
    inputs, specs, rows, entries, flops = [], [], 0, [], 0
    if returned is not None:
        parts, denominator = returned
        inputs += [parts, denominator]
        specs += [VMEM, VMEM]
        rows += returned_rows(parts.shape[1] // 8)
    if group is not None:
        first, left_split, rights = group
        arrays, entries = unique(rights)
        inputs += [first, left_split, *arrays]
        specs += [SMEM, VMEM] + [VMEM] * len(arrays)
        rows += 16 * len(entries)
        flops = len(entries) * 16 * TILE * TILE * left_split.shape[2]
    return pl.pallas_call(
        functools.partial(exchange_kernel, entries, returned is not None),
        out_shape=jax.ShapeDtypeStruct((TILE // 8, rows, TILE), jnp.float32),
        in_specs=specs,
        out_specs=VMEM,
        compiler_params=params(),
        cost_estimate=cost(flops, TILE // 8 * rows * TILE * 8),
        name="exchange",
    )(*inputs)


def unique(rights):
    arrays, entries = [], []
    for array, entry in rights:
        which = next((k for k, known in enumerate(arrays) if known is array), len(arrays))
        if which == len(arrays):
            arrays.append(array)
        entries.append((which, entry))
    return arrays, entries


def gamma_kernel(entries, carried, first_ref, amplitude_ref, *refs):
    if carried:
        gamma_in, *refs = refs
    *right_refs, gamma_ref, energy_ref = refs
    rows = gamma_ref.shape[0]
    count = 2 * len(entries)
    gamma_ref[...] = gamma_in[...] if carried else jnp.zeros_like(gamma_ref)
    for k, (which, entry) in enumerate(entries):
        for s in range(2):
            t = 2 * k + s
            value = amplitude_ref[:, 8 * t : 8 * t + 8, :].reshape(TILE, TILE)
            high, low = split(value)
            weights = jnp.concatenate(
                [
                    jnp.concatenate([high, high], axis=1),
                    jnp.concatenate([low, low], axis=1),
                ],
                axis=0,
            )
            both = jnp.concatenate(split(right_refs[which][entry, :, s * TILE : (s + 1) * TILE]), axis=1)
            part = lax.dot_general(both, weights, (((1,), (1,)), ((), ())), preferred_element_type=jnp.float32)
            place = lanes(first_ref[t])
            gamma_ref[:, place] += (part[:, :TILE] + part[:, TILE:])[:rows]
    energy_ref[...] = jnp.sum(amplitude_ref[:, 8 * count : 8 * count + energy_ref.shape[0], :], axis=0)


def gamma_add(first, amplitudes, rights, rows, cols, carried):
    arrays, entries = unique(rights)
    tiles = 2 * len(entries)
    inputs = (first, amplitudes) + ((carried,) if carried is not None else ())
    return pl.pallas_call(
        functools.partial(gamma_kernel, entries, carried is not None),
        out_shape=[
            jax.ShapeDtypeStruct((rows, cols), jnp.float32),
            jax.ShapeDtypeStruct((returned_rows(tiles) - 8 * tiles, TILE), jnp.float32),
        ],
        in_specs=[SMEM] + [VMEM] * (len(inputs) - 1 + len(arrays)),
        out_specs=[VMEM, VMEM],
        compiler_params=params(),
        cost_estimate=cost(tiles * 8 * TILE * TILE * rows, rows * cols * 8),
        name="gamma",
    )(*inputs, *arrays)


SHIFTS = ((0, 0), (0, 1), (1, 0), (3, 0), (1, 1), (3, 1), (2, 0), (2, 1))
GROUPS = (2, 4, 2)


def per_device(bq, eps_occ, eps_vir, tile_pairs, live_counts):
    occ_size = lax.axis_size("occ")
    me = lax.axis_index("occ")
    chip, core = me // 2, me % 2
    chips = occ_size // 2
    owner = lax.axis_index("aux")
    block = bq[0]
    rows, cols = block.shape
    padded = -(-rows // 16) * 16
    tile_count = cols // TILE
    own_pairs = tile_pairs[0, :, 0, :]
    all_pairs = lax.all_gather(own_pairs, "occ")

    def route(dx, dc):
        return [(x * 2 + c, (x + dx) % chips * 2 + (c + dc) % 2) for x in range(chips) for c in range(2)]

    def wanted(*shifts):
        receivers = jnp.stack([(chip + dx) % chips * 2 + (core + dc) % 2 for dx, dc in shifts])
        return (all_pairs[receivers, me] % tile_count).reshape(-1)

    def swapped(tiles):
        return lax.ppermute(tiles, "occ", route(0, 1))

    near_index = wanted((1, 0), (1, 1), (3, 0), (3, 1))
    ahead, behind = pick(near_index, block, (2, 2), padded)
    ahead = lax.ppermute(ahead, "occ", route(1, 0))
    behind = lax.ppermute(behind, "occ", route(3, 0))
    far_index = wanted((0, 0), (0, 1), (2, 0), (2, 1))
    own, mate, far = pick(far_index, block, (1, 1, 2), padded)
    mate = swapped(mate)
    left_split = left(block, padded)

    partners = jnp.stack([(chip - dx) % chips * 2 + (core - dc) % 2 for dx, dc in SHIFTS])
    chosen = own_pairs[partners]
    first = (chosen // tile_count).astype(jnp.int32)
    second = chosen % tile_count

    vir_rows = eps_vir.reshape(tile_count, TILE // 8, 8)[:, owner]
    vir_tiles = eps_vir.reshape(tile_count, TILE)
    pair_level = eps_occ[me] + eps_occ[partners]
    denominator = pair_level[:, None, None, None] - vir_rows[first][:, :, :, None] - vir_tiles[second][:, :, None, :]
    live = jnp.arange(2)[None, :] < live_counts[0][partners][:, None]
    denominator = jnp.where(live[:, :, None, None], denominator, jnp.inf)

    bounds = [sum(GROUPS[:g]) for g in range(len(GROUPS) + 1)]
    spans = [slice(a, b) for a, b in zip(bounds, bounds[1:])]
    places = [first[span].reshape(-1) for span in spans]
    levels = [denominator[span].reshape(-1, TILE) for span in spans]

    def sent(returned, group):
        return lax.all_to_all(exchange(returned, group), "aux", 0, 0)

    early_rights = [(own, 0), (mate, 0)]
    early_parts = sent(None, (places[0], left_split, early_rights))
    far, early_parts = lax.optimization_barrier((far, early_parts))
    far = lax.ppermute(far, "occ", route(2, 0))
    early = sent((early_parts, levels[0]), None)
    total, early_energy = gamma_add(places[0], early, early_rights, rows, cols, None)

    near_mate = swapped(jnp.stack([ahead[1], behind[1]]))
    near_rights = [(ahead, 0), (behind, 0), (near_mate, 0), (near_mate, 1)]
    near_place, early = lax.optimization_barrier((places[1], early))
    near_parts = sent(None, (near_place, left_split, near_rights))

    far_mate = swapped(far[1:])
    far_rights = [(far, 0), (far_mate, 0)]
    both = sent((near_parts, levels[1]), (places[2], left_split, far_rights))
    near_rows = returned_rows(2 * GROUPS[1])
    last = sent((both[:, near_rows:], levels[2]), None)
    total, near_energy = gamma_add(places[1], both, near_rights, rows, cols, total)
    total, last_energy = gamma_add(places[2], last, far_rights, rows, cols, total)

    energies = [
        jnp.sum(energy[: 2 * count].reshape(count, 2 * TILE), axis=1)
        for energy, count in zip((early_energy, near_energy, last_energy), GROUPS)
    ]
    mine = partners[:, None] == jnp.arange(occ_size)[None, :]
    energy = jnp.sum(jnp.where(mine, jnp.concatenate(energies)[:, None], 0.0), axis=0)
    energy = lax.psum(energy[None], "vir")
    return total[None], energy


def solution(mesh):
    return jax.shard_map(
        per_device,
        mesh=mesh,
        in_specs=(
            P("occ", "aux", "vir"),
            P(),
            P("vir"),
            P("occ", None, "vir", None),
            P("occ", None),
        ),
        out_specs=(P("occ", "aux", "vir"), P("occ", None)),
        check_vma=False,
    )
```

```python
import functools

import jax
import jax.numpy as jnp
from jax import lax
from jax.experimental import pallas as pl
from jax.experimental.pallas import tpu as pltpu
from jax.sharding import PartitionSpec as P

TILE = 128
CHIPS = 4
VMEM = pl.BlockSpec(memory_space=pltpu.VMEM)
SMEM = pl.BlockSpec(memory_space=pltpu.SMEM)
def params():
    return pltpu.CompilerParams(vmem_limit_bytes=12 * 1024 * 1024)


def cost(flops, moved):
    return pl.CostEstimate(flops=flops, bytes_accessed=moved, transcendentals=0)


def split(value):
    high = value.astype(jnp.bfloat16)
    low = (value - high.astype(jnp.float32)).astype(jnp.bfloat16)
    return high, low


def lanes(index):
    return pl.ds(pl.multiple_of(index * TILE, TILE), TILE)


def partner_of(ids_ref, dx, dc):
    me = ids_ref[0]
    return lax.rem(me // 2 + CHIPS - dx, CHIPS) * 2 + lax.rem(me + dc, 2)


def pick_kernel(shifts, ids_ref, pairs_ref, block_ref, *out_refs):
    rows, cols = block_ref.shape
    slots = [(out_ref, k) for out_ref in out_refs for k in range(out_ref.shape[0])]
    for (out_ref, k), (dx, dc) in zip(slots, shifts):
        receiver = partner_of(ids_ref, CHIPS - dx, dc)
        for s in range(2):
            tile = lax.rem(pairs_ref[(receiver * 2 * CHIPS + ids_ref[0]) * 2 + s], cols // TILE)
            out_ref[k, :rows, s * TILE : (s + 1) * TILE] = block_ref[:, lanes(tile)]
        out_ref[k, rows:, :] = jnp.zeros((out_ref.shape[1] - rows, 2 * TILE), jnp.float32)


def pick(ids, pairs, block, shifts, counts, padded):
    return pl.pallas_call(
        functools.partial(pick_kernel, shifts),
        out_shape=[jax.ShapeDtypeStruct((count, padded, 2 * TILE), jnp.float32) for count in counts],
        in_specs=[SMEM, SMEM, VMEM],
        out_specs=[VMEM] * len(counts),
        compiler_params=params(),
        cost_estimate=cost(0, sum(counts) * padded * 4 * TILE * 4),
        name="pick",
    )(ids, pairs, block)


def left_kernel(block_ref, out_ref):
    rows = block_ref.shape[0]
    padded = out_ref.shape[2]
    for f in range(out_ref.shape[0]):
        tile = block_ref[:, f * TILE : (f + 1) * TILE]
        tile = jnp.concatenate([tile, jnp.zeros((padded - rows, TILE), jnp.float32)], axis=0)
        high, low = split(tile.T)
        out_ref[f, :TILE, :] = high
        out_ref[f, TILE:, :] = low


def left(block, padded):
    tiles = block.shape[1] // TILE
    return pl.pallas_call(
        left_kernel,
        out_shape=jax.ShapeDtypeStruct((tiles, 2 * TILE, padded), jnp.bfloat16),
        in_specs=[VMEM],
        out_specs=VMEM,
        compiler_params=params(),
        cost_estimate=cost(0, block.size * 8),
        name="left",
    )(block)


def tiles_of(scalars, shift, s, tile_count):
    ids_ref, own_ref = scalars[:2]
    partner = partner_of(ids_ref, *shift)
    entry = own_ref[2 * partner + s]
    return partner, lax.div(entry, tile_count), lax.rem(entry, tile_count)


def add_amplitude(scalars, shifts, parts_ref, columns_ref, levels_ref, out_ref):
    ids_ref, _, occ_ref, live_ref = scalars
    count = 2 * len(shifts)
    energies = []
    for k, shift in enumerate(shifts):
        for s in range(2):
            t = 2 * k + s
            partner, first, second = tiles_of(scalars, shift, s, levels_ref.shape[0])
            row = pl.multiple_of(first * TILE + 8 * ids_ref[1], 8)
            denominator = (
                occ_ref[ids_ref[0]] + occ_ref[partner] - columns_ref[pl.ds(row, 8), :] - levels_ref[pl.ds(second, 1), :]
            )
            summed = jnp.sum(parts_ref[:, 8 * t : 8 * t + 8, :], axis=0)
            denominator = jnp.where(s < live_ref[partner], denominator, jnp.inf)
            amplitude = summed / denominator
            energies.append(jnp.sum(summed * amplitude, axis=0, keepdims=True))
            for owner in range(out_ref.shape[0]):
                out_ref[owner, 8 * t : 8 * t + 8, :] = amplitude
    energies.append(jnp.zeros((-count % 8, TILE), jnp.float32)) if count % 8 else None
    energy = jnp.concatenate(energies, axis=0)
    done = 8 * count + energy.shape[0]
    for owner in range(out_ref.shape[0]):
        out_ref[owner, 8 * count : done, :] = energy
    return done


def returned_rows(tiles):
    return 8 * tiles + -(-tiles // 8) * 8


def exchange_kernel(back_shifts, shifts, entries, *refs):
    *in_refs, out_ref = refs
    scalars, in_refs = in_refs[:4], in_refs[4:]
    at = 0
    if back_shifts:
        parts_ref, columns_ref, levels_ref, *in_refs = in_refs
        at = add_amplitude(scalars, back_shifts, parts_ref, columns_ref, levels_ref, out_ref)
    if entries:
        left_ref, *right_refs = in_refs
        for k, ((which, entry), shift) in enumerate(zip(entries, shifts)):
            for s in range(2):
                t = 2 * k + s
                _, first, _ = tiles_of(scalars, shift, s, left_ref.shape[0])
                high, low = split(right_refs[which][entry, :, s * TILE : (s + 1) * TILE])
                both = jnp.concatenate([high, low], axis=1)
                part = jnp.dot(left_ref[first], both, preferred_element_type=jnp.float32)
                cross = part[:TILE, TILE:] + part[TILE:, :TILE] + part[TILE:, TILE:]
                total = part[:TILE, :TILE] + cross
                out_ref[:, at + 8 * t : at + 8 * t + 8, :] = total.reshape(TILE // 8, 8, TILE)


def exchange(scalars, returned, group):
    inputs, specs, rows, flops = list(scalars), [SMEM] * 4, 0, 0
    back_shifts, shifts, entries = (), (), ()
    if returned is not None:
        back_shifts, parts, columns, levels = returned
        inputs += [parts, columns, levels]
        specs += [VMEM] * 3
        rows += returned_rows(2 * len(back_shifts))
    if group is not None:
        shifts, left_split, rights = group
        arrays, entries = unique(rights)
        inputs += [left_split, *arrays]
        specs += [VMEM] * (1 + len(arrays))
        rows += 16 * len(entries)
        flops = len(entries) * 16 * TILE * TILE * left_split.shape[2]
    return pl.pallas_call(
        functools.partial(exchange_kernel, back_shifts, shifts, entries),
        out_shape=jax.ShapeDtypeStruct((TILE // 8, rows, TILE), jnp.float32),
        in_specs=specs,
        out_specs=VMEM,
        compiler_params=params(),
        cost_estimate=cost(flops, TILE // 8 * rows * TILE * 8),
        name="exchange",
    )(*inputs)


def unique(rights):
    arrays, entries = [], []
    for array, entry in rights:
        which = next((k for k, known in enumerate(arrays) if known is array), len(arrays))
        if which == len(arrays):
            arrays.append(array)
        entries.append((which, entry))
    return arrays, entries


def gamma_kernel(groups, carried, *refs):
    scalars, refs = refs[:4], refs[4:]
    if carried:
        gamma_in, *refs = refs
    *in_refs, gamma_ref, energy_ref = refs
    rows, cols = gamma_ref.shape
    gamma_ref[...] = gamma_in[...] if carried else jnp.zeros_like(gamma_ref)
    energy_at = 0
    for shifts, entries, arrays in groups:
        (amplitude_ref, *right_refs), in_refs = in_refs[: 1 + arrays], in_refs[1 + arrays :]
        count = 2 * len(entries)
        for k, ((which, entry), shift) in enumerate(zip(entries, shifts)):
            for s in range(2):
                t = 2 * k + s
                _, first, _ = tiles_of(scalars, shift, s, cols // TILE)
                high, low = split(amplitude_ref[:, 8 * t : 8 * t + 8, :].reshape(TILE, TILE))
                weights = jnp.concatenate(
                    [
                        jnp.concatenate([high, high], axis=1),
                        jnp.concatenate([low, low], axis=1),
                    ],
                    axis=0,
                )
                both = jnp.concatenate(split(right_refs[which][entry, :, s * TILE : (s + 1) * TILE]), axis=1)
                part = lax.dot_general(both, weights, (((1,), (1,)), ((), ())), preferred_element_type=jnp.float32)
                place = lanes(first)
                gamma_ref[:, place] += (part[:, :TILE] + part[:, TILE:])[:rows]
        extra = returned_rows(count) - 8 * count
        energy = jnp.sum(amplitude_ref[:, 8 * count : 8 * count + extra, :], axis=0)
        energy_ref[energy_at : energy_at + extra, :] = energy
        energy_at += extra


def gamma_add(scalars, groups, rows, cols, carried):
    inputs, extra, tiles = [], 0, 0
    described = []
    for shifts, amplitudes, rights in groups:
        arrays, entries = unique(rights)
        described.append((shifts, entries, len(arrays)))
        inputs += [amplitudes, *arrays]
        extra += returned_rows(2 * len(shifts)) - 16 * len(shifts)
        tiles += 2 * len(shifts)
    start = list(scalars) + ([carried] if carried is not None else [])
    return pl.pallas_call(
        functools.partial(gamma_kernel, described, carried is not None),
        out_shape=[
            jax.ShapeDtypeStruct((rows, cols), jnp.float32),
            jax.ShapeDtypeStruct((extra, TILE), jnp.float32),
        ],
        in_specs=[SMEM] * 4 + [VMEM] * (len(start) - 4 + len(inputs)),
        out_specs=[VMEM, VMEM],
        compiler_params=params(),
        cost_estimate=cost(tiles * 8 * TILE * TILE * rows, rows * cols * 8),
        name="gamma",
    )(*start, *inputs)


EARLY = ((0, 0), (0, 1))
NEAR = ((1, 0), (3, 0), (1, 1), (3, 1))
FAR = ((2, 0), (2, 1))


def per_device(bq, eps_occ, eps_vir, tile_pairs, live_counts):
    occ_size = lax.axis_size("occ")
    me = lax.axis_index("occ")
    block = bq[0]
    rows, cols = block.shape
    padded = -(-rows // 16) * 16
    own_pairs = tile_pairs.reshape(-1)
    all_pairs = lax.all_gather(tile_pairs[0, :, 0, :], "occ").reshape(-1)
    ids = jnp.stack([me, lax.axis_index("aux")]).astype(jnp.int32)
    scalars = (ids, own_pairs, eps_occ, live_counts.reshape(-1))
    columns = jnp.broadcast_to(eps_vir[:, None], (cols, TILE))
    levels = eps_vir.reshape(cols // TILE, TILE)

    def route(dx, dc):
        return [(x * 2 + c, (x + dx) % CHIPS * 2 + (c + dc) % 2) for x in range(CHIPS) for c in range(2)]

    def swapped(tiles):
        return lax.ppermute(tiles, "occ", route(0, 1))

    def sent(returned, group):
        return lax.all_to_all(exchange(scalars, returned, group), "aux", 0, 0)

    ahead, behind = pick(ids, all_pairs, block, ((1, 0), (1, 1), (3, 0), (3, 1)), (2, 2), padded)
    ahead = lax.ppermute(ahead, "occ", route(1, 0))
    behind = lax.ppermute(behind, "occ", route(3, 0))
    own, mate, far = pick(ids, all_pairs, block, ((0, 0), (0, 1), (2, 0), (2, 1)), (1, 1, 2), padded)
    mate = swapped(mate)
    left_split = left(block, padded)

    early_rights = [(own, 0), (mate, 0)]
    early_parts = sent(None, (EARLY, left_split, early_rights))
    far, early_parts = lax.optimization_barrier((far, early_parts))
    far = lax.ppermute(far, "occ", route(2, 0))
    early = sent((EARLY, early_parts, columns, levels), None)

    near_mate = swapped(jnp.stack([ahead[1], behind[1]]))
    near_rights = [(ahead, 0), (behind, 0), (near_mate, 0), (near_mate, 1)]
    near_left, early = lax.optimization_barrier((left_split, early))
    near_parts = sent(None, (NEAR, near_left, near_rights))

    far_mate = swapped(far[1:])
    far_rights = [(far, 0), (far_mate, 0)]
    both = sent((NEAR, near_parts, columns, levels), (FAR, left_split, far_rights))
    near_rows = returned_rows(2 * len(NEAR))
    last = sent((FAR, both[:, near_rows:], columns, levels), None)
    total, energy = gamma_add(scalars, [(EARLY, early, early_rights), (NEAR, both, near_rights)], rows, cols, None)
    total, last_energy = gamma_add(scalars, [(FAR, last, far_rights)], rows, cols, total)

    energies = []
    for value, shifts, at in ((energy, EARLY, 0), (energy, NEAR, 8), (last_energy, FAR, 0)):
        pairs = value[at : at + 2 * len(shifts)].reshape(len(shifts), 2 * TILE)
        energies.append(jnp.sum(pairs, axis=1))
    order = jnp.stack([(me // 2 - dx) % CHIPS * 2 + (me + dc) % 2 for dx, dc in EARLY + NEAR + FAR])
    mine = order[:, None] == jnp.arange(occ_size)[None, :]
    energy = jnp.sum(jnp.where(mine, jnp.concatenate(energies)[:, None], 0.0), axis=0)
    energy = lax.psum(energy[None], "vir")
    return total[None], energy


def solution(mesh):
    return jax.shard_map(
        per_device,
        mesh=mesh,
        in_specs=(
            P("occ", "aux", "vir"),
            P(),
            P("vir"),
            P("occ", None, "vir", None),
            P("occ", None),
        ),
        out_specs=(P("occ", "aux", "vir"), P("occ", None)),
        check_vma=False,
    )
```

```python
import functools

import jax
import jax.numpy as jnp
from jax import lax
from jax.experimental import pallas as pl
from jax.experimental.pallas import tpu as pltpu
from jax.sharding import PartitionSpec as P

TILE = 128
CHIPS = 4
VMEM = pl.BlockSpec(memory_space=pltpu.VMEM)
SMEM = pl.BlockSpec(memory_space=pltpu.SMEM)
HBM = pl.BlockSpec(memory_space=pltpu.HBM)
def params():
    return pltpu.CompilerParams(vmem_limit_bytes=12 * 1024 * 1024)


def cost(flops, moved):
    return pl.CostEstimate(flops=flops, bytes_accessed=moved, transcendentals=0)


def split(value):
    high = value.astype(jnp.bfloat16)
    low = (value - high.astype(jnp.float32)).astype(jnp.bfloat16)
    return high, low


def lanes(index):
    return pl.ds(pl.multiple_of(index * TILE, TILE), TILE)


def partner_of(ids_ref, dx, dc):
    me = ids_ref[0]
    return lax.rem(me // 2 + CHIPS - dx, CHIPS) * 2 + lax.rem(me + dc, 2)


def pick_kernel(shifts, ids_ref, pairs_ref, block_ref, *refs):
    *out_refs, zeros_ref, sems = refs
    rows, cols = block_ref.shape
    slots = [(out_ref, k) for out_ref in out_refs for k in range(out_ref.shape[0])]
    zeros_ref[...] = jnp.zeros_like(zeros_ref)
    copies = []
    for (out_ref, k), (dx, dc) in zip(slots, shifts):
        receiver = partner_of(ids_ref, CHIPS - dx, dc)
        for s in range(2):
            tile = lax.rem(pairs_ref[(receiver * 2 * CHIPS + ids_ref[0]) * 2 + s], cols // TILE)
            source = block_ref.at[:, lanes(tile)]
            target = out_ref.at[k, pl.ds(0, rows), pl.ds(s * TILE, TILE)]
            copies.append(pltpu.make_async_copy(source, target, sems.at[len(copies)]))
        target = out_ref.at[k, pl.ds(rows, zeros_ref.shape[0]), :]
        copies.append(pltpu.make_async_copy(zeros_ref, target, sems.at[len(copies)]))
    for copy in copies:
        copy.start()
    for copy in copies:
        copy.wait()


def pick(ids, pairs, block, shifts, counts, padded):
    return pl.pallas_call(
        functools.partial(pick_kernel, shifts),
        out_shape=[jax.ShapeDtypeStruct((count, padded, 2 * TILE), jnp.float32) for count in counts],
        in_specs=[SMEM, SMEM, HBM],
        out_specs=[HBM] * len(counts),
        scratch_shapes=[
            pltpu.VMEM((padded - block.shape[0], 2 * TILE), jnp.float32),
            pltpu.SemaphoreType.DMA((3 * len(shifts),)),
        ],
        compiler_params=params(),
        cost_estimate=cost(0, sum(counts) * padded * 4 * TILE * 4),
        name="pick",
    )(ids, pairs, block)


def halves_kernel(*refs):
    *in_refs, out_ref, sems = refs
    copies = [pltpu.make_async_copy(ref.at[1], out_ref.at[k], sems.at[k]) for k, ref in enumerate(in_refs)]
    for copy in copies:
        copy.start()
    for copy in copies:
        copy.wait()


def halves(*arrays):
    return pl.pallas_call(
        halves_kernel,
        out_shape=jax.ShapeDtypeStruct((len(arrays), *arrays[0].shape[1:]), jnp.float32),
        in_specs=[HBM] * len(arrays),
        out_specs=HBM,
        scratch_shapes=[pltpu.SemaphoreType.DMA((len(arrays),))],
        compiler_params=params(),
        cost_estimate=cost(0, sum(array.size for array in arrays) * 4),
        name="halves",
    )(*arrays)


def left_kernel(block_ref, out_ref):
    rows = block_ref.shape[0]
    padded = out_ref.shape[2]
    for f in range(out_ref.shape[0]):
        tile = block_ref[:, f * TILE : (f + 1) * TILE]
        tile = jnp.concatenate([tile, jnp.zeros((padded - rows, TILE), jnp.float32)], axis=0)
        high, low = split(tile.T)
        out_ref[f, :TILE, :] = high
        out_ref[f, TILE:, :] = low


def left(block, padded):
    tiles = block.shape[1] // TILE
    return pl.pallas_call(
        left_kernel,
        out_shape=jax.ShapeDtypeStruct((tiles, 2 * TILE, padded), jnp.bfloat16),
        in_specs=[VMEM],
        out_specs=VMEM,
        compiler_params=params(),
        cost_estimate=cost(0, block.size * 8),
        name="left",
    )(block)


def tiles_of(scalars, shift, s, tile_count):
    ids_ref, own_ref = scalars[:2]
    partner = partner_of(ids_ref, *shift)
    entry = own_ref[2 * partner + s]
    return partner, lax.div(entry, tile_count), lax.rem(entry, tile_count)


def denominator_of(scalars, columns_ref, levels_ref, partner, first, second, start, count):
    ids_ref, _, occ_ref, _ = scalars
    row = pl.multiple_of(first * TILE + start, 8)
    occ = occ_ref[ids_ref[0]] + occ_ref[partner]
    return occ - columns_ref[pl.ds(row, count), :] - levels_ref[pl.ds(second, 1), :]


def add_amplitude(scalars, shifts, parts_at, parts_ref, columns_ref, levels_ref, out_ref):
    ids_ref, _, _, live_ref = scalars
    for k, shift in enumerate(shifts):
        for s in range(2):
            t = 2 * k + s
            partner, first, second = tiles_of(scalars, shift, s, levels_ref.shape[0])
            denominator = denominator_of(scalars, columns_ref, levels_ref, partner, first, second, 8 * ids_ref[1], 8)
            summed = jnp.sum(parts_ref[:, parts_at + 8 * t : parts_at + 8 * t + 8, :], axis=0)
            amplitude = summed / jnp.where(s < live_ref[partner], denominator, jnp.inf)
            for owner in range(out_ref.shape[0]):
                out_ref[owner, 8 * t : 8 * t + 8, :] = amplitude
    return 16 * len(shifts)


def exchange_kernel(back_shifts, parts_at, shifts, entries, *refs):
    *in_refs, out_ref = refs
    scalars, in_refs = in_refs[:4], in_refs[4:]
    at = 0
    if back_shifts:
        parts_ref, columns_ref, levels_ref, *in_refs = in_refs
        at = add_amplitude(scalars, back_shifts, parts_at, parts_ref, columns_ref, levels_ref, out_ref)
    if entries:
        left_ref, *right_refs = in_refs
        for k, ((which, entry), shift) in enumerate(zip(entries, shifts)):
            for s in range(2):
                t = 2 * k + s
                _, first, _ = tiles_of(scalars, shift, s, left_ref.shape[0])
                high, low = split(right_refs[which][entry, :, s * TILE : (s + 1) * TILE])
                both = jnp.concatenate([high, low], axis=1)
                part = jnp.dot(left_ref[first], both, preferred_element_type=jnp.float32)
                cross = part[:TILE, TILE:] + part[TILE:, :TILE] + part[TILE:, TILE:]
                total = part[:TILE, :TILE] + cross
                out_ref[:, at + 8 * t : at + 8 * t + 8, :] = total.reshape(TILE // 8, 8, TILE)


def exchange(scalars, returned, group):
    inputs, specs, rows, flops, parts_at = list(scalars), [SMEM] * 4, 0, 0, 0
    back_shifts, shifts, entries = (), (), ()
    if returned is not None:
        back_shifts, parts, parts_at, columns, levels = returned
        inputs += [parts, columns, levels]
        specs += [VMEM] * 3
        rows += 16 * len(back_shifts)
    if group is not None:
        shifts, left_split, rights = group
        arrays, entries = unique(rights)
        inputs += [left_split, *arrays]
        specs += [VMEM] * (1 + len(arrays))
        rows += 16 * len(entries)
        flops = len(entries) * 16 * TILE * TILE * left_split.shape[2]
    return pl.pallas_call(
        functools.partial(exchange_kernel, back_shifts, parts_at, shifts, entries),
        out_shape=jax.ShapeDtypeStruct((TILE // 8, rows, TILE), jnp.float32),
        in_specs=specs,
        out_specs=VMEM,
        compiler_params=params(),
        cost_estimate=cost(flops, TILE // 8 * rows * TILE * 8),
        name="exchange",
    )(*inputs)


def unique(rights):
    arrays, entries = [], []
    for array, entry in rights:
        which = next((k for k, known in enumerate(arrays) if known is array), len(arrays))
        if which == len(arrays):
            arrays.append(array)
        entries.append((which, entry))
    return arrays, entries


def tile_amplitude(amplitude_ref, t):
    return amplitude_ref[:, 8 * t : 8 * t + 8, :].reshape(TILE, TILE)


def energy_kernel(groups, *refs):
    scalars, (columns_ref, levels_ref, *amplitude_refs, out_ref) = refs[:4], refs[4:]
    rows = []
    for shifts, amplitude_ref in zip(groups, amplitude_refs):
        for k, shift in enumerate(shifts):
            for s in range(2):
                amplitude = tile_amplitude(amplitude_ref, 2 * k + s)
                place = tiles_of(scalars, shift, s, levels_ref.shape[0])
                denominator = denominator_of(scalars, columns_ref, levels_ref, *place, 0, TILE)
                rows.append(jnp.sum(amplitude * amplitude * denominator, axis=0, keepdims=True))
    for k in range(len(rows) // 2):
        out_ref[k : k + 1, :] = rows[2 * k] + rows[2 * k + 1]


def energy_of(scalars, columns, levels, groups):
    shifts = [group[0] for group in groups]
    partners = sum(len(group) for group in shifts)
    return pl.pallas_call(
        functools.partial(energy_kernel, shifts),
        out_shape=jax.ShapeDtypeStruct((partners, TILE), jnp.float32),
        in_specs=[SMEM] * 4 + [VMEM] * (2 + len(groups)),
        out_specs=VMEM,
        compiler_params=params(),
        cost_estimate=cost(6 * partners * TILE * TILE, partners * TILE * TILE * 8),
        name="energy",
    )(*scalars, columns, levels, *[group[1] for group in groups])


def gamma_kernel(groups, carried, *refs):
    scalars, refs = refs[:4], refs[4:]
    if carried:
        gamma_in, *refs = refs
    *in_refs, gamma_ref = refs
    rows, cols = gamma_ref.shape
    gamma_ref[...] = gamma_in[...] if carried else jnp.zeros_like(gamma_ref)
    for shifts, entries, arrays in groups:
        (amplitude_ref, *right_refs), in_refs = in_refs[: 1 + arrays], in_refs[1 + arrays :]
        for k, ((which, entry), shift) in enumerate(zip(entries, shifts)):
            for s in range(2):
                _, first, _ = tiles_of(scalars, shift, s, cols // TILE)
                high, low = split(tile_amplitude(amplitude_ref, 2 * k + s))
                weights = jnp.concatenate(
                    [
                        jnp.concatenate([high, high], axis=1),
                        jnp.concatenate([low, low], axis=1),
                    ],
                    axis=0,
                )
                both = jnp.concatenate(split(right_refs[which][entry, :, s * TILE : (s + 1) * TILE]), axis=1)
                part = lax.dot_general(both, weights, (((1,), (1,)), ((), ())), preferred_element_type=jnp.float32)
                place = lanes(first)
                gamma_ref[:, place] += (part[:, :TILE] + part[:, TILE:])[:rows]


def gamma_add(scalars, groups, rows, cols, carried):
    inputs, tiles, described = [], 0, []
    for shifts, amplitudes, rights in groups:
        arrays, entries = unique(rights)
        described.append((shifts, entries, len(arrays)))
        inputs += [amplitudes, *arrays]
        tiles += 2 * len(shifts)
    start = list(scalars) + ([carried] if carried is not None else [])
    return pl.pallas_call(
        functools.partial(gamma_kernel, described, carried is not None),
        out_shape=jax.ShapeDtypeStruct((rows, cols), jnp.float32),
        in_specs=[SMEM] * 4 + [VMEM] * (len(start) - 4 + len(inputs)),
        out_specs=VMEM,
        compiler_params=params(),
        cost_estimate=cost(tiles * 8 * TILE * TILE * rows, rows * cols * 8),
        name="gamma",
    )(*start, *inputs)


EARLY = ((0, 0), (0, 1))
NEAR = ((1, 0), (3, 0), (1, 1), (3, 1))
FAR = ((2, 0), (2, 1))


def per_device(bq, eps_occ, eps_vir, tile_pairs, live_counts):
    occ_size = lax.axis_size("occ")
    me = lax.axis_index("occ")
    block = bq[0]
    rows, cols = block.shape
    padded = -(-rows // 16) * 16
    own_pairs = tile_pairs.reshape(-1)
    all_pairs = lax.all_gather(tile_pairs[0, :, 0, :], "occ").reshape(-1)
    ids = jnp.stack([me, lax.axis_index("aux")]).astype(jnp.int32)
    scalars = (ids, own_pairs, eps_occ, live_counts.reshape(-1))
    columns = jnp.broadcast_to(eps_vir[:, None], (cols, TILE))
    levels = eps_vir.reshape(cols // TILE, TILE)

    def route(dx, dc):
        return [(x * 2 + c, (x + dx) % CHIPS * 2 + (c + dc) % 2) for x in range(CHIPS) for c in range(2)]

    def swapped(tiles):
        return lax.ppermute(tiles, "occ", route(0, 1))

    def sent(returned, group):
        return lax.all_to_all(exchange(scalars, returned, group), "aux", 0, 0)

    ahead, behind = pick(ids, all_pairs, block, ((1, 0), (1, 1), (3, 0), (3, 1)), (2, 2), padded)
    ahead = lax.ppermute(ahead, "occ", route(1, 0))
    behind = lax.ppermute(behind, "occ", route(3, 0))
    own, mate, far = pick(ids, all_pairs, block, ((0, 0), (0, 1), (2, 0), (2, 1)), (1, 1, 2), padded)
    mate = swapped(mate)
    left_split = left(block, padded)

    early_rights = [(own, 0), (mate, 0)]
    early_parts = sent(None, (EARLY, left_split, early_rights))
    far, ahead, behind, early_parts = lax.optimization_barrier((far, ahead, behind, early_parts))
    far = lax.ppermute(far, "occ", route(2, 0))
    near_mate = swapped(halves(ahead, behind))
    near_rights = [(ahead, 0), (behind, 0), (near_mate, 0), (near_mate, 1)]
    near = sent((EARLY, early_parts, 0, columns, levels), (NEAR, left_split, near_rights))

    far_mate = swapped(halves(far))
    far_rights = [(far, 0), (far_mate, 0)]
    both = sent((NEAR, near, 16 * len(EARLY), columns, levels), (FAR, left_split, far_rights))
    last = sent((FAR, both, 16 * len(NEAR), columns, levels), None)
    first_groups = [(EARLY, near, early_rights), (NEAR, both, near_rights)]
    total = gamma_add(scalars, first_groups, rows, cols, None)
    first_energy = energy_of(scalars, columns, levels, first_groups)
    last_energy = energy_of(scalars, columns, levels, [(FAR, last)])

    energy = jnp.sum(jnp.concatenate([first_energy, last_energy], axis=0), axis=1)
    for bit in (1, 2):
        blocks = range(lax.axis_size("vir"))
        energy = energy + lax.ppermute(energy, "vir", [(v, v ^ bit) for v in blocks])
    order = jnp.stack([(me // 2 - dx) % CHIPS * 2 + (me + dc) % 2 for dx, dc in EARLY + NEAR + FAR])
    mine = order[:, None] == jnp.arange(occ_size)[None, :]
    energy = jnp.sum(jnp.where(mine, energy[:, None], 0.0), axis=0)
    total = gamma_add(scalars, [(FAR, last, far_rights)], rows, cols, total)
    return total[None], energy[None]


def solution(mesh):
    return jax.shard_map(
        per_device,
        mesh=mesh,
        in_specs=(
            P("occ", "aux", "vir"),
            P(),
            P("vir"),
            P("occ", None, "vir", None),
            P("occ", None),
        ),
        out_specs=(P("occ", "aux", "vir"), P("occ", None)),
        check_vma=False,
    )
```

```python
import functools

import jax
import jax.numpy as jnp
from jax import lax
from jax.experimental import pallas as pl
from jax.experimental.pallas import tpu as pltpu
from jax.sharding import PartitionSpec as P

TILE = 128
CHIPS = 4
VMEM = pl.BlockSpec(memory_space=pltpu.VMEM)
SMEM = pl.BlockSpec(memory_space=pltpu.SMEM)
HBM = pl.BlockSpec(memory_space=pltpu.HBM)
def params():
    return pltpu.CompilerParams(vmem_limit_bytes=12 * 1024 * 1024)


def cost(flops, moved):
    return pl.CostEstimate(flops=flops, bytes_accessed=moved, transcendentals=0)


def split(value):
    high = value.astype(jnp.bfloat16)
    low = (value - high.astype(jnp.float32)).astype(jnp.bfloat16)
    return high, low


def lanes(index):
    return pl.ds(pl.multiple_of(index * TILE, TILE), TILE)


def partner_of(ids_ref, dx, dc):
    me = ids_ref[0]
    return lax.rem(me // 2 + CHIPS - dx, CHIPS) * 2 + lax.rem(me + dc, 2)


def pick_kernel(shifts, ids_ref, pairs_ref, block_ref, *refs):
    *out_refs, zeros_ref, sems = refs
    rows, cols = block_ref.shape
    slots = [(out_ref, k) for out_ref in out_refs for k in range(out_ref.shape[0])]
    zeros_ref[...] = jnp.zeros_like(zeros_ref)
    copies = []
    for (out_ref, k), (dx, dc) in zip(slots, shifts):
        receiver = partner_of(ids_ref, CHIPS - dx, dc)
        for s in range(2):
            tile = lax.rem(pairs_ref[(receiver * 2 * CHIPS + ids_ref[0]) * 2 + s], cols // TILE)
            source = block_ref.at[:, lanes(tile)]
            target = out_ref.at[k, pl.ds(0, rows), pl.ds(s * TILE, TILE)]
            copies.append(pltpu.make_async_copy(source, target, sems.at[len(copies)]))
        target = out_ref.at[k, pl.ds(rows, zeros_ref.shape[0]), :]
        copies.append(pltpu.make_async_copy(zeros_ref, target, sems.at[len(copies)]))
    for copy in copies:
        copy.start()
    for copy in copies:
        copy.wait()


def pick(ids, pairs, block, shifts, counts, padded):
    return pl.pallas_call(
        functools.partial(pick_kernel, shifts),
        out_shape=[jax.ShapeDtypeStruct((count, padded, 2 * TILE), jnp.float32) for count in counts],
        in_specs=[SMEM, SMEM, HBM],
        out_specs=[HBM] * len(counts),
        scratch_shapes=[
            pltpu.VMEM((padded - block.shape[0], 2 * TILE), jnp.float32),
            pltpu.SemaphoreType.DMA((3 * len(shifts),)),
        ],
        compiler_params=params(),
        cost_estimate=cost(0, sum(counts) * padded * 4 * TILE * 4),
        name="pick",
    )(ids, pairs, block)


def halves_kernel(*refs):
    *in_refs, out_ref, sems = refs
    copies = [pltpu.make_async_copy(ref.at[1], out_ref.at[k], sems.at[k]) for k, ref in enumerate(in_refs)]
    for copy in copies:
        copy.start()
    for copy in copies:
        copy.wait()


def halves(*arrays):
    return pl.pallas_call(
        halves_kernel,
        out_shape=jax.ShapeDtypeStruct((len(arrays), *arrays[0].shape[1:]), jnp.float32),
        in_specs=[HBM] * len(arrays),
        out_specs=HBM,
        scratch_shapes=[pltpu.SemaphoreType.DMA((len(arrays),))],
        compiler_params=params(),
        cost_estimate=cost(0, sum(array.size for array in arrays) * 4),
        name="halves",
    )(*arrays)


def left_kernel(block_ref, out_ref):
    rows = block_ref.shape[0]
    padded = out_ref.shape[2]
    for f in range(out_ref.shape[0]):
        tile = block_ref[:, f * TILE : (f + 1) * TILE]
        tile = jnp.concatenate([tile, jnp.zeros((padded - rows, TILE), jnp.float32)], axis=0)
        high, low = split(tile.T)
        out_ref[f, :TILE, :] = high
        out_ref[f, TILE:, :] = low


def left(block, padded):
    tiles = block.shape[1] // TILE
    return pl.pallas_call(
        left_kernel,
        out_shape=jax.ShapeDtypeStruct((tiles, 2 * TILE, padded), jnp.bfloat16),
        in_specs=[VMEM],
        out_specs=VMEM,
        compiler_params=params(),
        cost_estimate=cost(0, block.size * 8),
        name="left",
    )(block)


def tiles_of(scalars, shift, s, tile_count):
    ids_ref, own_ref = scalars[:2]
    partner = partner_of(ids_ref, *shift)
    entry = own_ref[2 * partner + s]
    return partner, lax.div(entry, tile_count), lax.rem(entry, tile_count)


def denominator_of(scalars, columns_ref, levels_ref, partner, first, second, start, count):
    ids_ref, _, occ_ref, _ = scalars
    row = pl.multiple_of(first * TILE + start, 8)
    occ = occ_ref[ids_ref[0]] + occ_ref[partner]
    return occ - columns_ref[pl.ds(row, count), :] - levels_ref[pl.ds(second, 1), :]


def add_amplitude(scalars, shifts, parts_at, parts_ref, columns_ref, levels_ref, out_ref, energy_ref):
    ids_ref, _, _, live_ref = scalars
    for k, shift in enumerate(shifts):
        energy = jnp.zeros((1, TILE), jnp.float32)
        for s in range(2):
            t = 2 * k + s
            partner, first, second = tiles_of(scalars, shift, s, levels_ref.shape[0])
            denominator = denominator_of(scalars, columns_ref, levels_ref, partner, first, second, 8 * ids_ref[1], 8)
            summed = jnp.sum(parts_ref[:, parts_at + 8 * t : parts_at + 8 * t + 8, :], axis=0)
            amplitude = summed / jnp.where(s < live_ref[partner], denominator, jnp.inf)
            energy = energy + jnp.sum(summed * amplitude, axis=0, keepdims=True)
            for owner in range(out_ref.shape[0]):
                out_ref[owner, 8 * t : 8 * t + 8, :] = amplitude
        energy_ref[k : k + 1, :] = energy
    return 16 * len(shifts)


def exchange_kernel(back_shifts, parts_at, shifts, entries, *refs):
    if back_shifts:
        *refs, energy_ref = refs
    *in_refs, out_ref = refs
    scalars, in_refs = in_refs[:4], in_refs[4:]
    at = 0
    if back_shifts:
        parts_ref, columns_ref, levels_ref, *in_refs = in_refs
        at = add_amplitude(scalars, back_shifts, parts_at, parts_ref, columns_ref, levels_ref, out_ref, energy_ref)
    if entries:
        left_ref, *right_refs = in_refs
        for k, ((which, entry), shift) in enumerate(zip(entries, shifts)):
            for s in range(2):
                t = 2 * k + s
                _, first, _ = tiles_of(scalars, shift, s, left_ref.shape[0])
                high, low = split(right_refs[which][entry, :, s * TILE : (s + 1) * TILE])
                both = jnp.concatenate([high, low], axis=1)
                part = jnp.dot(left_ref[first], both, preferred_element_type=jnp.float32)
                cross = part[:TILE, TILE:] + part[TILE:, :TILE] + part[TILE:, TILE:]
                total = part[:TILE, :TILE] + cross
                out_ref[:, at + 8 * t : at + 8 * t + 8, :] = total.reshape(TILE // 8, 8, TILE)


def exchange(scalars, returned, group):
    inputs, specs, rows, flops, parts_at = list(scalars), [SMEM] * 4, 0, 0, 0
    back_shifts, shifts, entries = (), (), ()
    if returned is not None:
        back_shifts, parts, parts_at, columns, levels = returned
        inputs += [parts, columns, levels]
        specs += [VMEM] * 3
        rows += 16 * len(back_shifts)
    if group is not None:
        shifts, left_split, rights = group
        arrays, entries = unique(rights)
        inputs += [left_split, *arrays]
        specs += [VMEM] * (1 + len(arrays))
        rows += 16 * len(entries)
        flops = len(entries) * 16 * TILE * TILE * left_split.shape[2]
    return pl.pallas_call(
        functools.partial(exchange_kernel, back_shifts, parts_at, shifts, entries),
        out_shape=[jax.ShapeDtypeStruct((TILE // 8, rows, TILE), jnp.float32)]
        + [jax.ShapeDtypeStruct((len(back_shifts), TILE), jnp.float32)] * bool(back_shifts),
        in_specs=specs,
        out_specs=[VMEM] * (1 + bool(back_shifts)),
        compiler_params=params(),
        cost_estimate=cost(flops, TILE // 8 * rows * TILE * 8),
        name="exchange",
    )(*inputs)


def unique(rights):
    arrays, entries = [], []
    for array, entry in rights:
        which = next((k for k, known in enumerate(arrays) if known is array), len(arrays))
        if which == len(arrays):
            arrays.append(array)
        entries.append((which, entry))
    return arrays, entries


def tile_amplitude(amplitude_ref, t):
    return amplitude_ref[:, 8 * t : 8 * t + 8, :].reshape(TILE, TILE)


def gamma_kernel(groups, carried, *refs):
    scalars, refs = refs[:4], refs[4:]
    if carried:
        gamma_in, *refs = refs
    *in_refs, gamma_ref = refs
    rows, cols = gamma_ref.shape
    gamma_ref[...] = gamma_in[...] if carried else jnp.zeros_like(gamma_ref)
    for shifts, entries, arrays in groups:
        (amplitude_ref, *right_refs), in_refs = in_refs[: 1 + arrays], in_refs[1 + arrays :]
        for k, ((which, entry), shift) in enumerate(zip(entries, shifts)):
            for s in range(2):
                _, first, _ = tiles_of(scalars, shift, s, cols // TILE)
                high, low = split(tile_amplitude(amplitude_ref, 2 * k + s))
                weights = jnp.concatenate(
                    [
                        jnp.concatenate([high, high], axis=1),
                        jnp.concatenate([low, low], axis=1),
                    ],
                    axis=0,
                )
                both = jnp.concatenate(split(right_refs[which][entry, :, s * TILE : (s + 1) * TILE]), axis=1)
                part = lax.dot_general(both, weights, (((1,), (1,)), ((), ())), preferred_element_type=jnp.float32)
                place = lanes(first)
                gamma_ref[:, place] += (part[:, :TILE] + part[:, TILE:])[:rows]


def gamma_add(scalars, groups, rows, cols, carried):
    inputs, tiles, described = [], 0, []
    for shifts, amplitudes, rights in groups:
        arrays, entries = unique(rights)
        described.append((shifts, entries, len(arrays)))
        inputs += [amplitudes, *arrays]
        tiles += 2 * len(shifts)
    start = list(scalars) + ([carried] if carried is not None else [])
    return pl.pallas_call(
        functools.partial(gamma_kernel, described, carried is not None),
        out_shape=jax.ShapeDtypeStruct((rows, cols), jnp.float32),
        in_specs=[SMEM] * 4 + [VMEM] * (len(start) - 4 + len(inputs)),
        out_specs=VMEM,
        compiler_params=params(),
        cost_estimate=cost(tiles * 8 * TILE * TILE * rows, rows * cols * 8),
        name="gamma",
    )(*start, *inputs)


EARLY = ((0, 0), (0, 1))
NEAR = ((1, 0), (3, 0))
CROSS = ((1, 1), (3, 1))
FAR = ((2, 0), (2, 1))


def per_device(bq, eps_occ, eps_vir, tile_pairs, live_counts):
    occ_size = lax.axis_size("occ")
    owners = lax.axis_size("aux")
    me = lax.axis_index("occ")
    block = bq[0]
    rows, cols = block.shape
    padded = -(-rows // 16) * 16
    own_pairs = tile_pairs.reshape(-1)
    all_pairs = lax.all_gather(tile_pairs[0, :, 0, :], "occ").reshape(-1)
    ids = jnp.stack([me, lax.axis_index("aux")]).astype(jnp.int32)
    scalars = (ids, own_pairs, eps_occ, live_counts.reshape(-1))
    columns = jnp.broadcast_to(eps_vir[:, None], (cols, TILE))
    levels = eps_vir.reshape(cols // TILE, TILE)

    def moved(tiles, dx, dc):
        route = [(x * 2 + c, (x + dx) % CHIPS * 2 + (c + dc) % 2) for x in range(CHIPS) for c in range(2)]
        return lax.ppermute(tiles, "occ", route)

    def sent(returned, group):
        if returned is not None:
            returned = (*returned, columns, levels)
        operand, *energy = exchange(scalars, returned, group)
        return lax.all_to_all(operand, "aux", 0, 0), *energy

    ahead, behind = pick(ids, all_pairs, block, ((1, 0), (1, 1), (3, 0), (3, 1)), (2, 2), padded)
    ahead, behind = moved(ahead, 1, 0), moved(behind, 3, 0)
    own, mate, far = pick(ids, all_pairs, block, EARLY + FAR, (1, 1, 2), padded)
    mate = moved(mate, 0, 1)
    left_split = left(block, padded)
    early_rights = [(own, 0), (mate, 0)]

    (first,) = sent(None, (EARLY, left_split, early_rights))
    far, ahead, behind, first = lax.optimization_barrier((far, ahead, behind, first))
    far = moved(far, 2, 0)
    near_rights = [(ahead, 0), (behind, 0)]
    cross_tiles = moved(halves(ahead, behind), 0, 1)
    cross_rights = [(cross_tiles, 0), (cross_tiles, 1)]
    back = 16 * len(EARLY)
    early, early_energy = sent((EARLY, first, 0), (NEAR, left_split, near_rights))
    near, near_energy = sent((NEAR, early, back), (CROSS, left_split, cross_rights))
    far_mate = moved(halves(far), 0, 1)
    far_rights = [(far, 0), (far_mate, 0)]
    cross, cross_energy = sent((CROSS, near, back), (FAR, left_split, far_rights))
    total = gamma_add(scalars, [(EARLY, early, early_rights), (NEAR, near, near_rights)], rows, cols, None)
    cross, total = lax.optimization_barrier((cross, total))
    last, last_energy = sent((FAR, cross, back), None)

    energy = jnp.concatenate([early_energy, near_energy, cross_energy, last_energy], axis=0)
    energy, last = lax.optimization_barrier((lax.psum(energy, "vir"), last))
    energy = lax.all_to_all(jnp.broadcast_to(energy, (owners, *energy.shape)), "aux", 0, 0)
    energy = jnp.sum(energy, axis=(0, 2))
    order = jnp.stack([(me // 2 - dx) % CHIPS * 2 + (me + dc) % 2 for dx, dc in EARLY + NEAR + CROSS + FAR])
    mine = order[:, None] == jnp.arange(occ_size)[None, :]
    energy = jnp.sum(jnp.where(mine, energy[:, None], 0.0), axis=0)
    total = gamma_add(scalars, [(CROSS, cross, cross_rights), (FAR, last, far_rights)], rows, cols, total)
    return total[None], energy[None]


def solution(mesh):
    return jax.shard_map(
        per_device,
        mesh=mesh,
        in_specs=(
            P("occ", "aux", "vir"),
            P(),
            P("vir"),
            P("occ", None, "vir", None),
            P("occ", None),
        ),
        out_specs=(P("occ", "aux", "vir"), P("occ", None)),
        check_vma=False,
    )
```

```python
import functools

import jax
import jax.numpy as jnp
from jax import lax
from jax.experimental import pallas as pl
from jax.experimental.pallas import tpu as pltpu
from jax.sharding import PartitionSpec as P

TILE = 128
CHIPS = 4
VMEM = pl.BlockSpec(memory_space=pltpu.VMEM)
SMEM = pl.BlockSpec(memory_space=pltpu.SMEM)
HBM = pl.BlockSpec(memory_space=pltpu.HBM)
def params():
    return pltpu.CompilerParams(vmem_limit_bytes=12 * 1024 * 1024)


def cost(flops, moved):
    return pl.CostEstimate(flops=flops, bytes_accessed=moved, transcendentals=0)


def split(value):
    high = value.astype(jnp.bfloat16)
    low = (value - high.astype(jnp.float32)).astype(jnp.bfloat16)
    return high, low


def lanes(index):
    return pl.ds(pl.multiple_of(index * TILE, TILE), TILE)


def partner_of(ids_ref, dx, dc):
    me = ids_ref[0]
    return lax.rem(me // 2 + CHIPS - dx, CHIPS) * 2 + lax.rem(me + dc, 2)


def pick_kernel(shifts, ids_ref, pairs_ref, block_ref, *refs):
    *out_refs, zeros_ref, sems = refs
    rows, cols = block_ref.shape
    slots = [(out_ref, k) for out_ref in out_refs for k in range(out_ref.shape[0])]
    zeros_ref[...] = jnp.zeros_like(zeros_ref)
    copies = []
    for (out_ref, k), (dx, dc) in zip(slots, shifts):
        receiver = partner_of(ids_ref, CHIPS - dx, dc)
        for s in range(2):
            tile = lax.rem(pairs_ref[(receiver * 2 * CHIPS + ids_ref[0]) * 2 + s], cols // TILE)
            source = block_ref.at[:, lanes(tile)]
            target = out_ref.at[k, pl.ds(0, rows), pl.ds(s * TILE, TILE)]
            copies.append(pltpu.make_async_copy(source, target, sems.at[len(copies)]))
        target = out_ref.at[k, pl.ds(rows, zeros_ref.shape[0]), :]
        copies.append(pltpu.make_async_copy(zeros_ref, target, sems.at[len(copies)]))
    for copy in copies:
        copy.start()
    for copy in copies:
        copy.wait()


def pick(ids, pairs, block, shifts, counts, padded):
    return pl.pallas_call(
        functools.partial(pick_kernel, shifts),
        out_shape=[jax.ShapeDtypeStruct((count, padded, 2 * TILE), jnp.float32) for count in counts],
        in_specs=[SMEM, SMEM, VMEM],
        out_specs=[HBM] * len(counts),
        scratch_shapes=[
            pltpu.VMEM((padded - block.shape[0], 2 * TILE), jnp.float32),
            pltpu.SemaphoreType.DMA((3 * len(shifts),)),
        ],
        compiler_params=params(),
        cost_estimate=cost(0, sum(counts) * padded * 4 * TILE * 4),
        name="pick",
    )(ids, pairs, block)


def held_kernel(*refs):
    del refs


def held(*arrays):
    return pl.pallas_call(
        held_kernel,
        out_shape=[jax.ShapeDtypeStruct(array.shape, array.dtype) for array in arrays],
        in_specs=[pl.BlockSpec(memory_space=pl.ANY)] * len(arrays),
        out_specs=[pl.BlockSpec(memory_space=pl.ANY)] * len(arrays),
        input_output_aliases={k: k for k in range(len(arrays))},
        compiler_params=params(),
        cost_estimate=cost(70 * 10**9, 70 * 3 * 10**6),
        name="held",
    )(*arrays)


def left_kernel(block_ref, out_ref):
    rows = block_ref.shape[0]
    padded = out_ref.shape[2]
    for f in range(out_ref.shape[0]):
        tile = block_ref[:, f * TILE : (f + 1) * TILE]
        tile = jnp.concatenate([tile, jnp.zeros((padded - rows, TILE), jnp.float32)], axis=0)
        high, low = split(tile.T)
        out_ref[f, :TILE, :] = high
        out_ref[f, TILE:, :] = low


def left(block, padded):
    tiles = block.shape[1] // TILE
    return pl.pallas_call(
        left_kernel,
        out_shape=jax.ShapeDtypeStruct((tiles, 2 * TILE, padded), jnp.bfloat16),
        in_specs=[VMEM],
        out_specs=VMEM,
        compiler_params=params(),
        cost_estimate=cost(0, block.size * 8),
        name="left",
    )(block)


def tiles_of(scalars, shift, s, tile_count):
    ids_ref, own_ref = scalars[:2]
    partner = partner_of(ids_ref, *shift)
    entry = own_ref[2 * partner + s]
    return partner, lax.div(entry, tile_count), lax.rem(entry, tile_count)


def denominator_of(scalars, columns_ref, levels_ref, partner, first, second, start, count):
    ids_ref, _, occ_ref, _ = scalars
    row = pl.multiple_of(first * TILE + start, 8)
    occ = occ_ref[ids_ref[0]] + occ_ref[partner]
    return occ - columns_ref[pl.ds(row, count), :] - levels_ref[pl.ds(second, 1), :]


def add_amplitude(scalars, shifts, parts_at, parts_ref, columns_ref, levels_ref, out_ref):
    ids_ref, _, _, live_ref = scalars
    for k, shift in enumerate(shifts):
        for s in range(2):
            t = 2 * k + s
            partner, first, second = tiles_of(scalars, shift, s, levels_ref.shape[0])
            denominator = denominator_of(scalars, columns_ref, levels_ref, partner, first, second, 8 * ids_ref[1], 8)
            summed = jnp.sum(parts_ref[:, parts_at + 8 * t : parts_at + 8 * t + 8, :], axis=0)
            amplitude = summed / jnp.where(s < live_ref[partner], denominator, jnp.inf)
            for owner in range(out_ref.shape[0]):
                out_ref[owner, 8 * t : 8 * t + 8, :] = amplitude
    return 16 * len(shifts)


def exchange_kernel(back_shifts, parts_at, shifts, entries, *refs):
    *in_refs, out_ref = refs
    scalars, in_refs = in_refs[:4], in_refs[4:]
    at = 0
    if back_shifts:
        parts_ref, columns_ref, levels_ref, *in_refs = in_refs
        at = add_amplitude(scalars, back_shifts, parts_at, parts_ref, columns_ref, levels_ref, out_ref)
    if entries:
        left_ref, *right_refs = in_refs
        for k, ((which, entry), shift) in enumerate(zip(entries, shifts)):
            for s in range(2):
                t = 2 * k + s
                _, first, _ = tiles_of(scalars, shift, s, left_ref.shape[0])
                high, low = split(right_refs[which][entry, :, s * TILE : (s + 1) * TILE])
                both = jnp.concatenate([high, low], axis=1)
                part = jnp.dot(left_ref[first], both, preferred_element_type=jnp.float32)
                cross = part[:TILE, TILE:] + part[TILE:, :TILE] + part[TILE:, TILE:]
                total = part[:TILE, :TILE] + cross
                out_ref[:, at + 8 * t : at + 8 * t + 8, :] = total.reshape(TILE // 8, 8, TILE)


def exchange(scalars, returned, group):
    inputs, specs, rows, flops, parts_at = list(scalars), [SMEM] * 4, 0, 0, 0
    back_shifts, shifts, entries = (), (), ()
    if returned is not None:
        back_shifts, parts, parts_at, columns, levels = returned
        inputs += [parts, columns, levels]
        specs += [VMEM] * 3
        rows += 16 * len(back_shifts)
    if group is not None:
        shifts, left_split, rights = group
        arrays, entries = unique(rights)
        inputs += [left_split, *arrays]
        specs += [VMEM] * (1 + len(arrays))
        rows += 16 * len(entries)
        flops = len(entries) * 16 * TILE * TILE * left_split.shape[2]
    return pl.pallas_call(
        functools.partial(exchange_kernel, back_shifts, parts_at, shifts, entries),
        out_shape=jax.ShapeDtypeStruct((TILE // 8, rows, TILE), jnp.float32),
        in_specs=specs,
        out_specs=VMEM,
        compiler_params=params(),
        cost_estimate=cost(flops, TILE // 8 * rows * TILE * 8),
        name="exchange",
    )(*inputs)


def unique(rights):
    arrays, entries = [], []
    for array, entry in rights:
        which = next((k for k, known in enumerate(arrays) if known is array), len(arrays))
        if which == len(arrays):
            arrays.append(array)
        entries.append((which, entry))
    return arrays, entries


def tile_amplitude(amplitude_ref, t):
    return amplitude_ref[:, 8 * t : 8 * t + 8, :].reshape(TILE, TILE)


def energy_kernel(groups, *refs):
    scalars, (columns_ref, levels_ref, *amplitude_refs, out_ref) = refs[:4], refs[4:]
    rows = []
    for shifts, amplitude_ref in zip(groups, amplitude_refs):
        for k, shift in enumerate(shifts):
            for s in range(2):
                amplitude = tile_amplitude(amplitude_ref, 2 * k + s)
                place = tiles_of(scalars, shift, s, levels_ref.shape[0])
                denominator = denominator_of(scalars, columns_ref, levels_ref, *place, 0, TILE)
                rows.append(jnp.sum(amplitude * amplitude * denominator, axis=0, keepdims=True))
    for k in range(len(rows) // 2):
        out_ref[k : k + 1, :] = rows[2 * k] + rows[2 * k + 1]


def energy_of(scalars, columns, levels, groups):
    shifts = [group[0] for group in groups]
    partners = sum(len(group) for group in shifts)
    return pl.pallas_call(
        functools.partial(energy_kernel, shifts),
        out_shape=jax.ShapeDtypeStruct((partners, TILE), jnp.float32),
        in_specs=[SMEM] * 4 + [VMEM] * (2 + len(groups)),
        out_specs=VMEM,
        compiler_params=params(),
        cost_estimate=cost(6 * partners * TILE * TILE, partners * TILE * TILE * 8),
        name="energy",
    )(*scalars, columns, levels, *[group[1] for group in groups])


def gamma_kernel(groups, carried, *refs):
    scalars, refs = refs[:4], refs[4:]
    if carried:
        gamma_in, *refs = refs
    *in_refs, gamma_ref = refs
    rows, cols = gamma_ref.shape
    gamma_ref[...] = gamma_in[...] if carried else jnp.zeros_like(gamma_ref)
    for shifts, entries, arrays in groups:
        (amplitude_ref, *right_refs), in_refs = in_refs[: 1 + arrays], in_refs[1 + arrays :]
        for k, ((which, entry), shift) in enumerate(zip(entries, shifts)):
            for s in range(2):
                _, first, _ = tiles_of(scalars, shift, s, cols // TILE)
                high, low = split(tile_amplitude(amplitude_ref, 2 * k + s))
                weights = jnp.concatenate(
                    [
                        jnp.concatenate([high, high], axis=1),
                        jnp.concatenate([low, low], axis=1),
                    ],
                    axis=0,
                )
                both = jnp.concatenate(split(right_refs[which][entry, :, s * TILE : (s + 1) * TILE]), axis=1)
                part = lax.dot_general(both, weights, (((1,), (1,)), ((), ())), preferred_element_type=jnp.float32)
                place = lanes(first)
                gamma_ref[:, place] += (part[:, :TILE] + part[:, TILE:])[:rows]


def gamma_add(scalars, groups, rows, cols, carried):
    inputs, tiles, described = [], 0, []
    for shifts, amplitudes, rights in groups:
        arrays, entries = unique(rights)
        described.append((shifts, entries, len(arrays)))
        inputs += [amplitudes, *arrays]
        tiles += 2 * len(shifts)
    start = list(scalars) + ([carried] if carried is not None else [])
    return pl.pallas_call(
        functools.partial(gamma_kernel, described, carried is not None),
        out_shape=jax.ShapeDtypeStruct((rows, cols), jnp.float32),
        in_specs=[SMEM] * 4 + [VMEM] * (len(start) - 4 + len(inputs)),
        out_specs=VMEM,
        compiler_params=params(),
        cost_estimate=cost(tiles * 8 * TILE * TILE * rows, rows * cols * 8),
        name="gamma",
    )(*start, *inputs)


NEAR = ((1, 0), (3, 0), (1, 1), (3, 1), (0, 1), (0, 0))
FAR = ((2, 0), (2, 1))


def per_device(bq, eps_occ, eps_vir, tile_pairs, live_counts):
    occ_size = lax.axis_size("occ")
    me = lax.axis_index("occ")
    block = bq[0]
    rows, cols = block.shape
    padded = -(-rows // 16) * 16
    own_pairs = tile_pairs.reshape(-1)
    all_pairs = lax.all_gather(tile_pairs[0, :, 0, :], "occ").reshape(-1)
    ids = jnp.stack([me, lax.axis_index("aux")]).astype(jnp.int32)
    scalars = (ids, own_pairs, eps_occ, live_counts.reshape(-1))
    columns = jnp.broadcast_to(eps_vir[:, None], (cols, TILE))
    levels = eps_vir.reshape(cols // TILE, TILE)

    def moved(tiles, dx, dc):
        route = [(x * 2 + c, (x + dx) % CHIPS * 2 + (c + dc) % 2) for x in range(CHIPS) for c in range(2)]
        return lax.ppermute(tiles, "occ", route)

    def sent(returned, group):
        return lax.all_to_all(exchange(scalars, returned, group), "aux", 0, 0)

    near = pick(ids, all_pairs, block, NEAR[:4], (1,) * 4, padded)
    later_ids, *near = lax.optimization_barrier((ids, *near))
    near = [moved(tiles, *shift) for tiles, shift in zip(near, NEAR)]
    mate, own, *far = pick(later_ids, all_pairs, block, NEAR[4:] + FAR, (1,) * 4, padded)
    mate = moved(mate, 0, 1)
    left_split = left(block, padded)
    *far, near[0], near[1] = lax.optimization_barrier((*far, near[0], near[1]))
    far = held(*[moved(tiles, *shift) for tiles, shift in zip(far, FAR)])
    near_rights = [(tiles, 0) for tiles in (*near, mate, own)]
    far_rights = [(tiles, 0) for tiles in far]

    parts = sent(None, (NEAR, left_split, near_rights))
    both = sent((NEAR, parts, 0, columns, levels), (FAR, left_split, far_rights))
    last = sent((FAR, both, 16 * len(NEAR), columns, levels), None)
    first_groups = [(NEAR, both, near_rights)]
    total = gamma_add(scalars, first_groups, rows, cols, None)
    first_energy = energy_of(scalars, columns, levels, first_groups)
    last_energy = energy_of(scalars, columns, levels, [(FAR, last)])

    energy = jnp.sum(jnp.concatenate([first_energy, last_energy], axis=0), axis=1)
    for bit in (1, 2):
        blocks = range(lax.axis_size("vir"))
        energy = energy + lax.ppermute(energy, "vir", [(v, v ^ bit) for v in blocks])
    order = jnp.stack([(me // 2 - dx) % CHIPS * 2 + (me + dc) % 2 for dx, dc in NEAR + FAR])
    mine = order[:, None] == jnp.arange(occ_size)[None, :]
    energy = jnp.sum(jnp.where(mine, energy[:, None], 0.0), axis=0)
    total = gamma_add(scalars, [(FAR, last, far_rights)], rows, cols, total)
    return total[None], energy[None]


def solution(mesh):
    return jax.shard_map(
        per_device,
        mesh=mesh,
        in_specs=(
            P("occ", "aux", "vir"),
            P(),
            P("vir"),
            P("occ", None, "vir", None),
            P("occ", None),
        ),
        out_specs=(P("occ", "aux", "vir"), P("occ", None)),
        check_vma=False,
    )
```

```python
import functools

import jax
import jax.numpy as jnp
from jax import lax
from jax.experimental import pallas as pl
from jax.experimental.pallas import tpu as pltpu
from jax.sharding import PartitionSpec as P

TILE = 128
CHIPS = 4
VMEM = pl.BlockSpec(memory_space=pltpu.VMEM)
SMEM = pl.BlockSpec(memory_space=pltpu.SMEM)
HBM = pl.BlockSpec(memory_space=pltpu.HBM)
def params():
    return pltpu.CompilerParams(vmem_limit_bytes=12 * 1024 * 1024)


def cost(flops, moved):
    return pl.CostEstimate(flops=flops, bytes_accessed=moved, transcendentals=0)


def split(value):
    high = value.astype(jnp.bfloat16)
    low = (value - high.astype(jnp.float32)).astype(jnp.bfloat16)
    return high, low


def lanes(index):
    return pl.ds(pl.multiple_of(index * TILE, TILE), TILE)


def partner_of(ids_ref, dx, dc):
    me = ids_ref[0]
    return lax.rem(me // 2 + CHIPS - dx, CHIPS) * 2 + lax.rem(me + dc, 2)


def pick_kernel(shifts, ids_ref, pairs_ref, block_ref, *refs):
    *out_refs, zeros_ref, sems = refs
    rows, cols = block_ref.shape
    slots = [(out_ref, k) for out_ref in out_refs for k in range(out_ref.shape[0])]
    zeros_ref[...] = jnp.zeros_like(zeros_ref)
    copies = []
    for (out_ref, k), (dx, dc) in zip(slots, shifts):
        receiver = partner_of(ids_ref, CHIPS - dx, dc)
        for s in range(2):
            tile = lax.rem(pairs_ref[(receiver * 2 * CHIPS + ids_ref[0]) * 2 + s], cols // TILE)
            source = block_ref.at[:, lanes(tile)]
            target = out_ref.at[k, pl.ds(0, rows), pl.ds(s * TILE, TILE)]
            copies.append(pltpu.make_async_copy(source, target, sems.at[len(copies)]))
        target = out_ref.at[k, pl.ds(rows, zeros_ref.shape[0]), :]
        copies.append(pltpu.make_async_copy(zeros_ref, target, sems.at[len(copies)]))
    for copy in copies:
        copy.start()
    for copy in copies:
        copy.wait()


def pick(ids, pairs, block, shifts, counts, padded):
    return pl.pallas_call(
        functools.partial(pick_kernel, shifts),
        out_shape=[jax.ShapeDtypeStruct((count, padded, 2 * TILE), jnp.float32) for count in counts],
        in_specs=[SMEM, SMEM, VMEM],
        out_specs=[HBM] * len(counts),
        scratch_shapes=[
            pltpu.VMEM((padded - block.shape[0], 2 * TILE), jnp.float32),
            pltpu.SemaphoreType.DMA((3 * len(shifts),)),
        ],
        compiler_params=params(),
        cost_estimate=cost(0, sum(counts) * padded * 4 * TILE * 4),
        name="pick",
    )(ids, pairs, block)


def held_kernel(*refs):
    del refs


def held(*arrays):
    return pl.pallas_call(
        held_kernel,
        out_shape=[jax.ShapeDtypeStruct(array.shape, array.dtype) for array in arrays],
        in_specs=[pl.BlockSpec(memory_space=pl.ANY)] * len(arrays),
        out_specs=[pl.BlockSpec(memory_space=pl.ANY)] * len(arrays),
        input_output_aliases={k: k for k in range(len(arrays))},
        compiler_params=params(),
        cost_estimate=cost(70 * 10**9, 70 * 3 * 10**6),
        name="held",
    )(*arrays)


def left_kernel(block_ref, out_ref):
    rows = block_ref.shape[0]
    padded = out_ref.shape[2]
    for f in range(out_ref.shape[0]):
        tile = block_ref[:, f * TILE : (f + 1) * TILE]
        tile = jnp.concatenate([tile, jnp.zeros((padded - rows, TILE), jnp.float32)], axis=0)
        high, low = split(tile.T)
        out_ref[f, :TILE, :] = high
        out_ref[f, TILE:, :] = low


def left(block, padded):
    tiles = block.shape[1] // TILE
    return pl.pallas_call(
        left_kernel,
        out_shape=jax.ShapeDtypeStruct((tiles, 2 * TILE, padded), jnp.bfloat16),
        in_specs=[VMEM],
        out_specs=VMEM,
        compiler_params=params(),
        cost_estimate=cost(0, block.size * 8),
        name="left",
    )(block)


def tiles_of(scalars, shift, s, tile_count):
    ids_ref, own_ref = scalars[:2]
    partner = partner_of(ids_ref, *shift)
    entry = own_ref[2 * partner + s]
    return partner, lax.div(entry, tile_count), lax.rem(entry, tile_count)


def denominator_of(scalars, columns_ref, levels_ref, partner, first, second, start, count):
    ids_ref, _, occ_ref, _ = scalars
    row = pl.multiple_of(first * TILE + start, 8)
    occ = occ_ref[ids_ref[0]] + occ_ref[partner]
    return occ - columns_ref[pl.ds(row, count), :] - levels_ref[pl.ds(second, 1), :]


def add_amplitude(scalars, shifts, parts_at, parts_ref, columns_ref, levels_ref, out_ref):
    ids_ref, _, _, live_ref = scalars
    for k, shift in enumerate(shifts):
        for s in range(2):
            t = 2 * k + s
            partner, first, second = tiles_of(scalars, shift, s, levels_ref.shape[0])
            denominator = denominator_of(scalars, columns_ref, levels_ref, partner, first, second, 8 * ids_ref[1], 8)
            summed = jnp.sum(parts_ref[:, parts_at + 8 * t : parts_at + 8 * t + 8, :], axis=0)
            amplitude = summed / jnp.where(s < live_ref[partner], denominator, jnp.inf)
            for owner in range(out_ref.shape[0]):
                out_ref[owner, 8 * t : 8 * t + 8, :] = amplitude
    return 16 * len(shifts)


def exchange_kernel(back_shifts, parts_at, shifts, entries, *refs):
    *in_refs, out_ref = refs
    scalars, in_refs = in_refs[:4], in_refs[4:]
    at = 0
    if back_shifts:
        parts_ref, columns_ref, levels_ref, *in_refs = in_refs
        at = add_amplitude(scalars, back_shifts, parts_at, parts_ref, columns_ref, levels_ref, out_ref)
    if entries:
        left_ref, *right_refs = in_refs
        for k, ((which, entry), shift) in enumerate(zip(entries, shifts)):
            for s in range(2):
                t = 2 * k + s
                _, first, _ = tiles_of(scalars, shift, s, left_ref.shape[0])
                high, low = split(right_refs[which][entry, :, s * TILE : (s + 1) * TILE])
                both = jnp.concatenate([high, low], axis=1)
                part = jnp.dot(left_ref[first], both, preferred_element_type=jnp.float32)
                cross = part[:TILE, TILE:] + part[TILE:, :TILE] + part[TILE:, TILE:]
                total = part[:TILE, :TILE] + cross
                out_ref[:, at + 8 * t : at + 8 * t + 8, :] = total.reshape(TILE // 8, 8, TILE)


def exchange(scalars, returned, group):
    inputs, specs, rows, flops, parts_at = list(scalars), [SMEM] * 4, 0, 0, 0
    back_shifts, shifts, entries = (), (), ()
    if returned is not None:
        back_shifts, parts, parts_at, columns, levels = returned
        inputs += [parts, columns, levels]
        specs += [VMEM] * 3
        rows += 16 * len(back_shifts)
    if group is not None:
        shifts, left_split, rights = group
        arrays, entries = unique(rights)
        inputs += [left_split, *arrays]
        specs += [VMEM] * (1 + len(arrays))
        rows += 16 * len(entries)
        flops = len(entries) * 16 * TILE * TILE * left_split.shape[2]
    return pl.pallas_call(
        functools.partial(exchange_kernel, back_shifts, parts_at, shifts, entries),
        out_shape=jax.ShapeDtypeStruct((TILE // 8, rows, TILE), jnp.float32),
        in_specs=specs,
        out_specs=VMEM,
        compiler_params=params(),
        cost_estimate=cost(flops, TILE // 8 * rows * TILE * 8),
        name="exchange",
    )(*inputs)


def unique(rights):
    arrays, entries = [], []
    for array, entry in rights:
        which = next((k for k, known in enumerate(arrays) if known is array), len(arrays))
        if which == len(arrays):
            arrays.append(array)
        entries.append((which, entry))
    return arrays, entries


def tile_amplitude(amplitude_ref, t):
    return amplitude_ref[:, 8 * t : 8 * t + 8, :].reshape(TILE, TILE)


def energy_kernel(groups, *refs):
    scalars, (columns_ref, levels_ref, *amplitude_refs, out_ref) = refs[:4], refs[4:]
    rows = []
    for shifts, amplitude_ref in zip(groups, amplitude_refs):
        for k, shift in enumerate(shifts):
            for s in range(2):
                amplitude = tile_amplitude(amplitude_ref, 2 * k + s)
                place = tiles_of(scalars, shift, s, levels_ref.shape[0])
                denominator = denominator_of(scalars, columns_ref, levels_ref, *place, 0, TILE)
                rows.append(jnp.sum(amplitude * amplitude * denominator, axis=0, keepdims=True))
    for k in range(len(rows) // 2):
        out_ref[k : k + 1, :] = rows[2 * k] + rows[2 * k + 1]


def energy_of(scalars, columns, levels, groups):
    shifts = [group[0] for group in groups]
    partners = sum(len(group) for group in shifts)
    return pl.pallas_call(
        functools.partial(energy_kernel, shifts),
        out_shape=jax.ShapeDtypeStruct((partners, TILE), jnp.float32),
        in_specs=[SMEM] * 4 + [VMEM] * (2 + len(groups)),
        out_specs=VMEM,
        compiler_params=params(),
        cost_estimate=cost(6 * partners * TILE * TILE, partners * TILE * TILE * 8),
        name="energy",
    )(*scalars, columns, levels, *[group[1] for group in groups])


def gamma_kernel(groups, carried, *refs):
    scalars, refs = refs[:4], refs[4:]
    if carried:
        gamma_in, *refs = refs
    *in_refs, gamma_ref = refs
    rows, cols = gamma_ref.shape
    gamma_ref[...] = gamma_in[...] if carried else jnp.zeros_like(gamma_ref)
    for shifts, entries, arrays in groups:
        (amplitude_ref, *right_refs), in_refs = in_refs[: 1 + arrays], in_refs[1 + arrays :]
        for k, ((which, entry), shift) in enumerate(zip(entries, shifts)):
            for s in range(2):
                _, first, _ = tiles_of(scalars, shift, s, cols // TILE)
                high, low = split(tile_amplitude(amplitude_ref, 2 * k + s))
                weights = jnp.concatenate(
                    [
                        jnp.concatenate([high, high], axis=1),
                        jnp.concatenate([low, low], axis=1),
                    ],
                    axis=0,
                )
                both = jnp.concatenate(split(right_refs[which][entry, :, s * TILE : (s + 1) * TILE]), axis=1)
                part = lax.dot_general(both, weights, (((1,), (1,)), ((), ())), preferred_element_type=jnp.float32)
                place = lanes(first)
                gamma_ref[:, place] += (part[:, :TILE] + part[:, TILE:])[:rows]


def gamma_add(scalars, groups, rows, cols, carried):
    inputs, tiles, described = [], 0, []
    for shifts, amplitudes, rights in groups:
        arrays, entries = unique(rights)
        described.append((shifts, entries, len(arrays)))
        inputs += [amplitudes, *arrays]
        tiles += 2 * len(shifts)
    start = list(scalars) + ([carried] if carried is not None else [])
    return pl.pallas_call(
        functools.partial(gamma_kernel, described, carried is not None),
        out_shape=jax.ShapeDtypeStruct((rows, cols), jnp.float32),
        in_specs=[SMEM] * 4 + [VMEM] * (len(start) - 4 + len(inputs)),
        out_specs=VMEM,
        compiler_params=params(),
        cost_estimate=cost(tiles * 8 * TILE * TILE * rows, rows * cols * 8),
        name="gamma",
    )(*start, *inputs)


NEAR = ((1, 0), (3, 0), (1, 1), (3, 1), (0, 1), (0, 0))
FAR = ((2, 0), (2, 1))


def per_device(bq, eps_occ, eps_vir, tile_pairs, live_counts):
    occ_size = lax.axis_size("occ")
    me = lax.axis_index("occ")
    block = bq[0]
    rows, cols = block.shape
    padded = -(-rows // 16) * 16
    own_pairs = tile_pairs.reshape(-1)
    all_pairs = lax.all_gather(tile_pairs[0, :, 0, :], "occ").reshape(-1)
    ids = jnp.stack([me, lax.axis_index("aux")]).astype(jnp.int32)
    scalars = (ids, own_pairs, eps_occ, live_counts.reshape(-1))
    columns = jnp.broadcast_to(eps_vir[:, None], (cols, TILE))
    levels = eps_vir.reshape(cols // TILE, TILE)

    def moved(tiles, dx, dc):
        route = [(x * 2 + c, (x + dx) % CHIPS * 2 + (c + dc) % 2) for x in range(CHIPS) for c in range(2)]
        return lax.ppermute(tiles, "occ", route)

    def sent(returned, group):
        return lax.all_to_all(exchange(scalars, returned, group), "aux", 0, 0)

    near = pick(ids, all_pairs, block, NEAR[:4], (1,) * 4, padded)
    later_ids, *near = lax.optimization_barrier((ids, *near))
    near = [moved(tiles, *shift) for tiles, shift in zip(near, NEAR)]
    mate, own, *far = pick(later_ids, all_pairs, block, NEAR[4:] + FAR, (1,) * 4, padded)
    mate = moved(mate, 0, 1)
    left_split = left(block, padded)
    far[0], far[1], left_split, *near = lax.optimization_barrier((*far, left_split, *near))
    far = held(*[moved(tiles, *shift) for tiles, shift in zip(far, FAR)])
    near_rights = [(tiles, 0) for tiles in (*near, mate, own)]
    far_rights = [(tiles, 0) for tiles in far]

    parts = sent(None, (NEAR, left_split, near_rights))
    both = sent((NEAR, parts, 0, columns, levels), (FAR, left_split, far_rights))
    last = sent((FAR, both, 16 * len(NEAR), columns, levels), None)
    first_groups = [(NEAR, both, near_rights)]
    total = gamma_add(scalars, first_groups, rows, cols, None)
    first_energy = energy_of(scalars, columns, levels, first_groups)
    last, total, first_energy = lax.optimization_barrier((last, total, first_energy))
    last_energy = energy_of(scalars, columns, levels, [(FAR, last)])

    energy = jnp.sum(jnp.concatenate([first_energy, last_energy], axis=0), axis=1)
    energy, last = lax.optimization_barrier((lax.psum(energy, "vir"), last))
    order = jnp.stack([(me // 2 - dx) % CHIPS * 2 + (me + dc) % 2 for dx, dc in NEAR + FAR])
    mine = order[:, None] == jnp.arange(occ_size)[None, :]
    energy = jnp.sum(jnp.where(mine, energy[:, None], 0.0), axis=0)
    total = gamma_add(scalars, [(FAR, last, far_rights)], rows, cols, total)
    return total[None], energy[None]


def solution(mesh):
    return jax.shard_map(
        per_device,
        mesh=mesh,
        in_specs=(
            P("occ", "aux", "vir"),
            P(),
            P("vir"),
            P("occ", None, "vir", None),
            P("occ", None),
        ),
        out_specs=(P("occ", "aux", "vir"), P("occ", None)),
        check_vma=False,
    )
```

```python
import functools

import jax
import jax.numpy as jnp
from jax import lax
from jax.experimental import pallas as pl
from jax.experimental.pallas import tpu as pltpu
from jax.sharding import PartitionSpec as P

TILE = 128
CHIPS = 4
VMEM = pl.BlockSpec(memory_space=pltpu.VMEM)
SMEM = pl.BlockSpec(memory_space=pltpu.SMEM)
HBM = pl.BlockSpec(memory_space=pltpu.HBM)
def params():
    return pltpu.CompilerParams(vmem_limit_bytes=12 * 1024 * 1024)


def cost(flops, moved):
    return pl.CostEstimate(flops=flops, bytes_accessed=moved, transcendentals=0)


def split(value):
    high = value.astype(jnp.bfloat16)
    low = (value - high.astype(jnp.float32)).astype(jnp.bfloat16)
    return high, low


def lanes(index):
    return pl.ds(pl.multiple_of(index * TILE, TILE), TILE)


def partner_of(ids_ref, dx, dc):
    me = ids_ref[0]
    return lax.rem(me // 2 + CHIPS - dx, CHIPS) * 2 + lax.rem(me + dc, 2)


def pick_kernel(shifts, ids_ref, pairs_ref, block_ref, *refs):
    *out_refs, zeros_ref, sems = refs
    rows, cols = block_ref.shape
    slots = [(out_ref, k) for out_ref in out_refs for k in range(out_ref.shape[0])]
    zeros_ref[...] = jnp.zeros_like(zeros_ref)
    copies = []
    for (out_ref, k), (dx, dc) in zip(slots, shifts):
        receiver = partner_of(ids_ref, CHIPS - dx, dc)
        for s in range(2):
            tile = lax.rem(pairs_ref[receiver, ids_ref[0] * 2 + s], cols // TILE)
            source = block_ref.at[:, lanes(tile)]
            target = out_ref.at[k, pl.ds(0, rows), pl.ds(s * TILE, TILE)]
            copies.append(pltpu.make_async_copy(source, target, sems.at[len(copies)]))
        target = out_ref.at[k, pl.ds(rows, zeros_ref.shape[0]), :]
        copies.append(pltpu.make_async_copy(zeros_ref, target, sems.at[len(copies)]))
    for copy in copies:
        copy.start()
    for copy in copies:
        copy.wait()


def pick(ids, pairs, block, shifts, counts, padded):
    return pl.pallas_call(
        functools.partial(pick_kernel, shifts),
        out_shape=[jax.ShapeDtypeStruct((count, padded, 2 * TILE), jnp.float32) for count in counts],
        in_specs=[SMEM, SMEM, VMEM],
        out_specs=[HBM] * len(counts),
        scratch_shapes=[
            pltpu.VMEM((padded - block.shape[0], 2 * TILE), jnp.float32),
            pltpu.SemaphoreType.DMA((3 * len(shifts),)),
        ],
        compiler_params=params(),
        cost_estimate=cost(0, sum(counts) * padded * 4 * TILE * 4),
        name="pick",
    )(ids, pairs, block)


def held_kernel(*refs):
    del refs


def held(hint, *arrays):
    return pl.pallas_call(
        held_kernel,
        out_shape=[jax.ShapeDtypeStruct(array.shape, array.dtype) for array in arrays],
        in_specs=[pl.BlockSpec(memory_space=pl.ANY)] * len(arrays),
        out_specs=[pl.BlockSpec(memory_space=pl.ANY)] * len(arrays),
        input_output_aliases={k: k for k in range(len(arrays))},
        compiler_params=params(),
        cost_estimate=cost(hint * 10**9, hint * 3 * 10**6),
        name="held",
    )(*arrays)


def left_kernel(block_ref, out_ref):
    rows = block_ref.shape[0]
    padded = out_ref.shape[2]
    for f in range(out_ref.shape[0]):
        tile = block_ref[:, f * TILE : (f + 1) * TILE]
        tile = jnp.concatenate([tile, jnp.zeros((padded - rows, TILE), jnp.float32)], axis=0)
        high, low = split(tile.T)
        out_ref[f, :TILE, :] = high
        out_ref[f, TILE:, :] = low


def left(block, padded):
    tiles = block.shape[1] // TILE
    return pl.pallas_call(
        left_kernel,
        out_shape=jax.ShapeDtypeStruct((tiles, 2 * TILE, padded), jnp.bfloat16),
        in_specs=[VMEM],
        out_specs=VMEM,
        compiler_params=params(),
        cost_estimate=cost(0, block.size * 8),
        name="left",
    )(block)


def tiles_of(scalars, shift, s, tile_count):
    ids_ref, own_ref = scalars[:2]
    partner = partner_of(ids_ref, *shift)
    entry = own_ref[2 * partner + s]
    return partner, lax.div(entry, tile_count), lax.rem(entry, tile_count)


def denominator_of(scalars, columns_ref, levels_ref, partner, first, second, start, count):
    ids_ref, _, occ_ref, _ = scalars
    row = pl.multiple_of(first * TILE + start, 8)
    occ = occ_ref[ids_ref[0]] + occ_ref[partner]
    return occ - columns_ref[pl.ds(row, count), :] - levels_ref[pl.ds(second, 1), :]


def add_amplitude(scalars, shifts, parts_at, parts_ref, columns_ref, levels_ref, out_ref):
    ids_ref, _, _, live_ref = scalars
    for k, shift in enumerate(shifts):
        for s in range(2):
            t = 2 * k + s
            partner, first, second = tiles_of(scalars, shift, s, levels_ref.shape[0])
            denominator = denominator_of(scalars, columns_ref, levels_ref, partner, first, second, 8 * ids_ref[1], 8)
            summed = jnp.sum(parts_ref[:, parts_at + 8 * t : parts_at + 8 * t + 8, :], axis=0)
            amplitude = summed / jnp.where(s < live_ref[partner], denominator, jnp.inf)
            for owner in range(out_ref.shape[0]):
                out_ref[owner, 8 * t : 8 * t + 8, :] = amplitude
    return 16 * len(shifts)


def exchange_kernel(back_shifts, parts_at, shifts, entries, *refs):
    *in_refs, out_ref = refs
    scalars, in_refs = in_refs[:4], in_refs[4:]
    at = 0
    if back_shifts:
        parts_ref, columns_ref, levels_ref, *in_refs = in_refs
        at = add_amplitude(scalars, back_shifts, parts_at, parts_ref, columns_ref, levels_ref, out_ref)
    if entries:
        left_ref, *right_refs = in_refs
        for k, ((which, entry), shift) in enumerate(zip(entries, shifts)):
            for s in range(2):
                t = 2 * k + s
                _, first, _ = tiles_of(scalars, shift, s, left_ref.shape[0])
                high, low = split(right_refs[which][entry, :, s * TILE : (s + 1) * TILE])
                both = jnp.concatenate([high, low], axis=1)
                part = jnp.dot(left_ref[first], both, preferred_element_type=jnp.float32)
                cross = part[:TILE, TILE:] + part[TILE:, :TILE] + part[TILE:, TILE:]
                total = part[:TILE, :TILE] + cross
                out_ref[:, at + 8 * t : at + 8 * t + 8, :] = total.reshape(TILE // 8, 8, TILE)


def exchange(scalars, returned, group):
    inputs, specs, rows, flops, parts_at = list(scalars), [SMEM] * 4, 0, 0, 0
    back_shifts, shifts, entries = (), (), ()
    if returned is not None:
        back_shifts, parts, parts_at, columns, levels = returned
        inputs += [parts, columns, levels]
        specs += [VMEM] * 3
        rows += 16 * len(back_shifts)
    if group is not None:
        shifts, left_split, rights = group
        arrays, entries = unique(rights)
        inputs += [left_split, *arrays]
        specs += [VMEM] * (1 + len(arrays))
        rows += 16 * len(entries)
        flops = len(entries) * 16 * TILE * TILE * left_split.shape[2]
    return pl.pallas_call(
        functools.partial(exchange_kernel, back_shifts, parts_at, shifts, entries),
        out_shape=jax.ShapeDtypeStruct((TILE // 8, rows, TILE), jnp.float32),
        in_specs=specs,
        out_specs=VMEM,
        compiler_params=params(),
        cost_estimate=cost(flops, TILE // 8 * rows * TILE * 8),
        name="exchange",
    )(*inputs)


def unique(rights):
    arrays, entries = [], []
    for array, entry in rights:
        which = next((k for k, known in enumerate(arrays) if known is array), len(arrays))
        if which == len(arrays):
            arrays.append(array)
        entries.append((which, entry))
    return arrays, entries


def tile_amplitude(amplitude_ref, t):
    return amplitude_ref[:, 8 * t : 8 * t + 8, :].reshape(TILE, TILE)


def energy_kernel(groups, *refs):
    scalars, (columns_ref, levels_ref, *amplitude_refs, out_ref) = refs[:4], refs[4:]
    rows = []
    for shifts, amplitude_ref in zip(groups, amplitude_refs):
        for k, shift in enumerate(shifts):
            for s in range(2):
                amplitude = tile_amplitude(amplitude_ref, 2 * k + s)
                place = tiles_of(scalars, shift, s, levels_ref.shape[0])
                denominator = denominator_of(scalars, columns_ref, levels_ref, *place, 0, TILE)
                rows.append(jnp.sum(amplitude * amplitude * denominator, axis=0, keepdims=True))
    for k in range(len(rows) // 2):
        out_ref[k : k + 1, :] = rows[2 * k] + rows[2 * k + 1]


def energy_of(scalars, columns, levels, groups):
    shifts = [group[0] for group in groups]
    partners = sum(len(group) for group in shifts)
    return pl.pallas_call(
        functools.partial(energy_kernel, shifts),
        out_shape=jax.ShapeDtypeStruct((partners, TILE), jnp.float32),
        in_specs=[SMEM] * 4 + [VMEM] * (2 + len(groups)),
        out_specs=VMEM,
        compiler_params=params(),
        cost_estimate=cost(6 * partners * TILE * TILE, partners * TILE * TILE * 8),
        name="energy",
    )(*scalars, columns, levels, *[group[1] for group in groups])


def gamma_kernel(groups, carried, *refs):
    scalars, refs = refs[:4], refs[4:]
    if carried:
        gamma_in, *refs = refs
    *in_refs, gamma_ref = refs
    rows, cols = gamma_ref.shape
    gamma_ref[...] = gamma_in[...] if carried else jnp.zeros_like(gamma_ref)
    for shifts, entries, arrays in groups:
        (amplitude_ref, *right_refs), in_refs = in_refs[: 1 + arrays], in_refs[1 + arrays :]
        for k, ((which, entry), shift) in enumerate(zip(entries, shifts)):
            for s in range(2):
                _, first, _ = tiles_of(scalars, shift, s, cols // TILE)
                high, low = split(tile_amplitude(amplitude_ref, 2 * k + s))
                weights = jnp.concatenate(
                    [
                        jnp.concatenate([high, high], axis=1),
                        jnp.concatenate([low, low], axis=1),
                    ],
                    axis=0,
                )
                both = jnp.concatenate(split(right_refs[which][entry, :, s * TILE : (s + 1) * TILE]), axis=1)
                part = lax.dot_general(both, weights, (((1,), (1,)), ((), ())), preferred_element_type=jnp.float32)
                place = lanes(first)
                gamma_ref[:, place] += (part[:, :TILE] + part[:, TILE:])[:rows]


def gamma_add(scalars, groups, rows, cols, carried):
    inputs, tiles, described = [], 0, []
    for shifts, amplitudes, rights in groups:
        arrays, entries = unique(rights)
        described.append((shifts, entries, len(arrays)))
        inputs += [amplitudes, *arrays]
        tiles += 2 * len(shifts)
    start = list(scalars) + ([carried] if carried is not None else [])
    return pl.pallas_call(
        functools.partial(gamma_kernel, described, carried is not None),
        out_shape=jax.ShapeDtypeStruct((rows, cols), jnp.float32),
        in_specs=[SMEM] * 4 + [VMEM] * (len(start) - 4 + len(inputs)),
        out_specs=VMEM,
        compiler_params=params(),
        cost_estimate=cost(tiles * 8 * TILE * TILE * rows, rows * cols * 8),
        name="gamma",
    )(*start, *inputs)


NEAR = ((1, 0), (3, 0), (1, 1), (3, 1), (0, 1))
FAR = ((2, 0), (2, 1), (0, 0))


def per_device(bq, eps_occ, eps_vir, tile_pairs, live_counts):
    occ_size = lax.axis_size("occ")
    me = lax.axis_index("occ")
    block = bq[0]
    rows, cols = block.shape
    padded = -(-rows // 16) * 16
    own_pairs = tile_pairs.reshape(-1)
    all_pairs = lax.all_gather(own_pairs, "occ")
    ids = jnp.stack([me, lax.axis_index("aux")]).astype(jnp.int32)
    scalars = (ids, own_pairs, eps_occ, live_counts.reshape(-1))
    columns = jnp.broadcast_to(eps_vir[:, None], (cols, TILE))
    levels = eps_vir.reshape(cols // TILE, TILE)

    def moved(tiles, dx, dc):
        route = [(x * 2 + c, (x + dx) % CHIPS * 2 + (c + dc) % 2) for x in range(CHIPS) for c in range(2)]
        return lax.ppermute(tiles, "occ", route)

    def sent(returned, group):
        return lax.all_to_all(exchange(scalars, returned, group), "aux", 0, 0)

    near = pick(ids, all_pairs, block, NEAR[:4], (1,) * 4, padded)
    later_ids, *near = lax.optimization_barrier((ids, *near))
    near = [moved(tiles, *shift) for tiles, shift in zip(near, NEAR)]
    mate, *far, own = pick(later_ids, all_pairs, block, NEAR[4:] + FAR, (1,) * 4, padded)
    mate = moved(mate, 0, 1)
    left_split = left(block, padded)
    far[0], far[1], left_split, *near = lax.optimization_barrier((*far, left_split, *near))
    near_rights = [(tiles, 0) for tiles in (*near, mate)]
    operand = exchange(scalars, None, (NEAR, left_split, near_rights))
    far[1], operand = lax.optimization_barrier((far[1], operand))
    far = [held(hint, moved(tiles, *shift))[0] for hint, tiles, shift in zip((70, 8), far, FAR)]
    far_rights = [(tiles, 0) for tiles in (*far, own)]

    parts = lax.all_to_all(operand, "aux", 0, 0)
    both = sent((NEAR, parts, 0, columns, levels), (FAR, left_split, far_rights))
    last = sent((FAR, both, 16 * len(NEAR), columns, levels), None)
    first_groups = [(NEAR, both, near_rights)]
    total = gamma_add(scalars, first_groups, rows, cols, None)
    first_energy = energy_of(scalars, columns, levels, first_groups)
    last, total, first_energy = lax.optimization_barrier((last, total, first_energy))
    last_energy = energy_of(scalars, columns, levels, [(FAR, last)])

    energy = jnp.sum(jnp.concatenate([first_energy, last_energy], axis=0), axis=1)
    energy, last = lax.optimization_barrier((lax.psum(energy, "vir"), last))
    order = jnp.stack([(me // 2 - dx) % CHIPS * 2 + (me + dc) % 2 for dx, dc in NEAR + FAR])
    mine = order[:, None] == jnp.arange(occ_size)[None, :]
    energy = jnp.sum(jnp.where(mine, energy[:, None], 0.0), axis=0)
    total = gamma_add(scalars, [(FAR, last, far_rights)], rows, cols, total)
    return total[None], energy[None]


def solution(mesh):
    return jax.shard_map(
        per_device,
        mesh=mesh,
        in_specs=(
            P("occ", "aux", "vir"),
            P(),
            P("vir"),
            P("occ", None, "vir", None),
            P("occ", None),
        ),
        out_specs=(P("occ", "aux", "vir"), P("occ", None)),
        check_vma=False,
    )
```

```python
import functools

import jax
import jax.numpy as jnp
from jax import lax
from jax.experimental import pallas as pl
from jax.experimental.pallas import tpu as pltpu
from jax.sharding import PartitionSpec as P

TILE = 128
CHIPS = 4
VMEM = pl.BlockSpec(memory_space=pltpu.VMEM)
SMEM = pl.BlockSpec(memory_space=pltpu.SMEM)
HBM = pl.BlockSpec(memory_space=pltpu.HBM)
def params():
    return pltpu.CompilerParams(vmem_limit_bytes=12 * 1024 * 1024)


def cost(flops, moved):
    return pl.CostEstimate(flops=flops, bytes_accessed=moved, transcendentals=0)


def split(value):
    high = value.astype(jnp.bfloat16)
    low = (value - high.astype(jnp.float32)).astype(jnp.bfloat16)
    return high, low


def lanes(index):
    return pl.ds(pl.multiple_of(index * TILE, TILE), TILE)


def partner_of(ids_ref, dx, dc):
    me = ids_ref[0]
    return lax.rem(me // 2 + CHIPS - dx, CHIPS) * 2 + lax.rem(me + dc, 2)


def pick_kernel(shifts, ids_ref, pairs_ref, block_ref, *refs):
    *out_refs, zeros_ref, sems = refs
    rows, cols = block_ref.shape
    slots = [(out_ref, k) for out_ref in out_refs for k in range(out_ref.shape[0])]
    zeros_ref[...] = jnp.zeros_like(zeros_ref)
    copies = []
    for (out_ref, k), (dx, dc) in zip(slots, shifts):
        receiver = partner_of(ids_ref, CHIPS - dx, dc)
        for s in range(2):
            tile = lax.rem(pairs_ref[(receiver * 2 * CHIPS + ids_ref[0]) * 2 + s], cols // TILE)
            source = block_ref.at[:, lanes(tile)]
            target = out_ref.at[k, pl.ds(0, rows), pl.ds(s * TILE, TILE)]
            copies.append(pltpu.make_async_copy(source, target, sems.at[len(copies)]))
        target = out_ref.at[k, pl.ds(rows, zeros_ref.shape[0]), :]
        copies.append(pltpu.make_async_copy(zeros_ref, target, sems.at[len(copies)]))
    for copy in copies:
        copy.start()
    for copy in copies:
        copy.wait()


def pick(ids, pairs, block, shifts, counts, padded):
    return pl.pallas_call(
        functools.partial(pick_kernel, shifts),
        out_shape=[jax.ShapeDtypeStruct((count, padded, 2 * TILE), jnp.float32) for count in counts],
        in_specs=[SMEM, SMEM, VMEM],
        out_specs=[HBM] * len(counts),
        scratch_shapes=[
            pltpu.VMEM((padded - block.shape[0], 2 * TILE), jnp.float32),
            pltpu.SemaphoreType.DMA((3 * len(shifts),)),
        ],
        compiler_params=params(),
        cost_estimate=cost(0, sum(counts) * padded * 4 * TILE * 4),
        name="pick",
    )(ids, pairs, block)


def held_kernel(*refs):
    del refs


def held(hint, *arrays):
    return pl.pallas_call(
        held_kernel,
        out_shape=[jax.ShapeDtypeStruct(array.shape, array.dtype) for array in arrays],
        in_specs=[pl.BlockSpec(memory_space=pl.ANY)] * len(arrays),
        out_specs=[pl.BlockSpec(memory_space=pl.ANY)] * len(arrays),
        input_output_aliases={k: k for k in range(len(arrays))},
        compiler_params=params(),
        cost_estimate=cost(hint * 10**9, hint * 3 * 10**6),
        name="held",
    )(*arrays)


def left_kernel(block_ref, out_ref):
    rows = block_ref.shape[0]
    padded = out_ref.shape[2]
    for f in range(out_ref.shape[0]):
        tile = block_ref[:, f * TILE : (f + 1) * TILE]
        tile = jnp.concatenate([tile, jnp.zeros((padded - rows, TILE), jnp.float32)], axis=0)
        high, low = split(tile.T)
        out_ref[f, :TILE, :] = high
        out_ref[f, TILE:, :] = low


def left(block, padded):
    tiles = block.shape[1] // TILE
    return pl.pallas_call(
        left_kernel,
        out_shape=jax.ShapeDtypeStruct((tiles, 2 * TILE, padded), jnp.bfloat16),
        in_specs=[VMEM],
        out_specs=VMEM,
        compiler_params=params(),
        cost_estimate=cost(0, block.size * 8),
        name="left",
    )(block)


def tiles_of(scalars, shift, s, tile_count):
    ids_ref, own_ref = scalars[:2]
    partner = partner_of(ids_ref, *shift)
    entry = own_ref[2 * partner + s]
    return partner, lax.div(entry, tile_count), lax.rem(entry, tile_count)


def denominator_of(scalars, columns_ref, levels_ref, partner, first, second, start, count):
    ids_ref, _, occ_ref, _ = scalars
    row = pl.multiple_of(first * TILE + start, 8)
    occ = occ_ref[ids_ref[0]] + occ_ref[partner]
    return occ - columns_ref[pl.ds(row, count), :] - levels_ref[pl.ds(second, 1), :]


def add_amplitude(scalars, shifts, parts_at, parts_ref, columns_ref, levels_ref, out_ref):
    ids_ref, _, _, live_ref = scalars
    for k, shift in enumerate(shifts):
        for s in range(2):
            t = 2 * k + s
            partner, first, second = tiles_of(scalars, shift, s, levels_ref.shape[0])
            denominator = denominator_of(scalars, columns_ref, levels_ref, partner, first, second, 8 * ids_ref[1], 8)
            summed = jnp.sum(parts_ref[:, parts_at + 8 * t : parts_at + 8 * t + 8, :], axis=0)
            amplitude = summed / jnp.where(s < live_ref[partner], denominator, jnp.inf)
            for owner in range(out_ref.shape[0]):
                out_ref[owner, 8 * t : 8 * t + 8, :] = amplitude
    return 16 * len(shifts)


def exchange_kernel(back_shifts, parts_at, shifts, entries, *refs):
    *in_refs, out_ref = refs
    scalars, in_refs = in_refs[:4], in_refs[4:]
    at = 0
    if back_shifts:
        parts_ref, columns_ref, levels_ref, *in_refs = in_refs
        at = add_amplitude(scalars, back_shifts, parts_at, parts_ref, columns_ref, levels_ref, out_ref)
    if entries:
        left_ref, *right_refs = in_refs
        for k, ((which, entry), shift) in enumerate(zip(entries, shifts)):
            for s in range(2):
                t = 2 * k + s
                _, first, _ = tiles_of(scalars, shift, s, left_ref.shape[0])
                high, low = split(right_refs[which][entry, :, s * TILE : (s + 1) * TILE])
                both = jnp.concatenate([high, low], axis=1)
                part = jnp.dot(left_ref[first], both, preferred_element_type=jnp.float32)
                cross = part[:TILE, TILE:] + part[TILE:, :TILE] + part[TILE:, TILE:]
                total = part[:TILE, :TILE] + cross
                out_ref[:, at + 8 * t : at + 8 * t + 8, :] = total.reshape(TILE // 8, 8, TILE)


def exchange(scalars, returned, group):
    inputs, specs, rows, flops, parts_at = list(scalars), [SMEM] * 4, 0, 0, 0
    back_shifts, shifts, entries = (), (), ()
    if returned is not None:
        back_shifts, parts, parts_at, columns, levels = returned
        inputs += [parts, columns, levels]
        specs += [VMEM] * 3
        rows += 16 * len(back_shifts)
    if group is not None:
        shifts, left_split, rights = group
        arrays, entries = unique(rights)
        inputs += [left_split, *arrays]
        specs += [VMEM] * (1 + len(arrays))
        rows += 16 * len(entries)
        flops = len(entries) * 16 * TILE * TILE * left_split.shape[2]
    return pl.pallas_call(
        functools.partial(exchange_kernel, back_shifts, parts_at, shifts, entries),
        out_shape=jax.ShapeDtypeStruct((TILE // 8, rows, TILE), jnp.float32),
        in_specs=specs,
        out_specs=VMEM,
        compiler_params=params(),
        cost_estimate=cost(flops, TILE // 8 * rows * TILE * 8),
        name="exchange",
    )(*inputs)


def unique(rights):
    arrays, entries = [], []
    for array, entry in rights:
        which = next((k for k, known in enumerate(arrays) if known is array), len(arrays))
        if which == len(arrays):
            arrays.append(array)
        entries.append((which, entry))
    return arrays, entries


def tile_amplitude(amplitude_ref, t):
    return amplitude_ref[:, 8 * t : 8 * t + 8, :].reshape(TILE, TILE)


def energy_kernel(groups, *refs):
    scalars, (columns_ref, levels_ref, *amplitude_refs, out_ref) = refs[:4], refs[4:]
    rows = []
    for shifts, amplitude_ref in zip(groups, amplitude_refs):
        for k, shift in enumerate(shifts):
            for s in range(2):
                amplitude = tile_amplitude(amplitude_ref, 2 * k + s)
                place = tiles_of(scalars, shift, s, levels_ref.shape[0])
                denominator = denominator_of(scalars, columns_ref, levels_ref, *place, 0, TILE)
                rows.append(jnp.sum(amplitude * amplitude * denominator, axis=0, keepdims=True))
    for k in range(len(rows) // 2):
        out_ref[k : k + 1, :] = rows[2 * k] + rows[2 * k + 1]


def energy_of(scalars, columns, levels, groups):
    shifts = [group[0] for group in groups]
    partners = sum(len(group) for group in shifts)
    return pl.pallas_call(
        functools.partial(energy_kernel, shifts),
        out_shape=jax.ShapeDtypeStruct((partners, TILE), jnp.float32),
        in_specs=[SMEM] * 4 + [VMEM] * (2 + len(groups)),
        out_specs=VMEM,
        compiler_params=params(),
        cost_estimate=cost(6 * partners * TILE * TILE, partners * TILE * TILE * 8),
        name="energy",
    )(*scalars, columns, levels, *[group[1] for group in groups])


def gamma_kernel(groups, carried, *refs):
    scalars, refs = refs[:4], refs[4:]
    if carried:
        gamma_in, *refs = refs
    *in_refs, gamma_ref = refs
    rows, cols = gamma_ref.shape
    gamma_ref[...] = gamma_in[...] if carried else jnp.zeros_like(gamma_ref)
    for shifts, entries, arrays in groups:
        (amplitude_ref, *right_refs), in_refs = in_refs[: 1 + arrays], in_refs[1 + arrays :]
        for k, ((which, entry), shift) in enumerate(zip(entries, shifts)):
            for s in range(2):
                _, first, _ = tiles_of(scalars, shift, s, cols // TILE)
                high, low = split(tile_amplitude(amplitude_ref, 2 * k + s))
                weights = jnp.concatenate(
                    [
                        jnp.concatenate([high, high], axis=1),
                        jnp.concatenate([low, low], axis=1),
                    ],
                    axis=0,
                )
                both = jnp.concatenate(split(right_refs[which][entry, :, s * TILE : (s + 1) * TILE]), axis=1)
                part = lax.dot_general(both, weights, (((1,), (1,)), ((), ())), preferred_element_type=jnp.float32)
                place = lanes(first)
                gamma_ref[:, place] += (part[:, :TILE] + part[:, TILE:])[:rows]


def gamma_add(scalars, groups, rows, cols, carried):
    inputs, tiles, described = [], 0, []
    for shifts, amplitudes, rights in groups:
        arrays, entries = unique(rights)
        described.append((shifts, entries, len(arrays)))
        inputs += [amplitudes, *arrays]
        tiles += 2 * len(shifts)
    start = list(scalars) + ([carried] if carried is not None else [])
    return pl.pallas_call(
        functools.partial(gamma_kernel, described, carried is not None),
        out_shape=jax.ShapeDtypeStruct((rows, cols), jnp.float32),
        in_specs=[SMEM] * 4 + [VMEM] * (len(start) - 4 + len(inputs)),
        out_specs=VMEM,
        compiler_params=params(),
        cost_estimate=cost(tiles * 8 * TILE * TILE * rows, rows * cols * 8),
        name="gamma",
    )(*start, *inputs)


EARLY = ((0, 1), (0, 0))
NEAR = ((1, 0), (3, 0), (1, 1), (3, 1))
FAR = ((2, 0), (2, 1))


def per_device(bq, eps_occ, eps_vir, tile_pairs, live_counts):
    occ_size = lax.axis_size("occ")
    me = lax.axis_index("occ")
    block = bq[0]
    rows, cols = block.shape
    padded = -(-rows // 16) * 16
    own_pairs = tile_pairs.reshape(-1)
    all_pairs = lax.all_gather(tile_pairs[0, :, 0, :], "occ").reshape(-1)
    ids = jnp.stack([me, lax.axis_index("aux")]).astype(jnp.int32)
    scalars = (ids, own_pairs, eps_occ, live_counts.reshape(-1))
    columns = jnp.broadcast_to(eps_vir[:, None], (cols, TILE))
    levels = eps_vir.reshape(cols // TILE, TILE)

    def moved(tiles, dx, dc):
        route = [(x * 2 + c, (x + dx) % CHIPS * 2 + (c + dc) % 2) for x in range(CHIPS) for c in range(2)]
        return lax.ppermute(tiles, "occ", route)

    def sent(returned, group):
        return lax.all_to_all(exchange(scalars, returned, group), "aux", 0, 0)

    near = pick(ids, all_pairs, block, NEAR, (1,) * 4, padded)
    later_ids, *near = lax.optimization_barrier((ids, *near))
    near = held(70, *[moved(tiles, *shift) for tiles, shift in zip(near, NEAR)])
    mate, own, *far = pick(later_ids, all_pairs, block, EARLY + FAR, (1,) * 4, padded)
    early_rights = [(moved(mate, 0, 1), 0), (own, 0)]
    left_split = left(block, padded)

    early = sent(None, (EARLY, left_split, early_rights))
    far[0], far[1], early, *near = lax.optimization_barrier((*far, early, *near))
    far = held(70, *[moved(tiles, *shift) for tiles, shift in zip(far, FAR)])
    near_rights = [(tiles, 0) for tiles in near]
    far_rights = [(tiles, 0) for tiles in far]

    parts = sent((EARLY, early, 0, columns, levels), (NEAR, left_split, near_rights))
    both = sent((NEAR, parts, 16 * len(EARLY), columns, levels), (FAR, left_split, far_rights))
    last = sent((FAR, both, 16 * len(NEAR), columns, levels), None)
    first_groups = [(EARLY, parts, early_rights), (NEAR, both, near_rights)]
    total = gamma_add(scalars, first_groups, rows, cols, None)
    first_energy = energy_of(scalars, columns, levels, first_groups)
    last, total, first_energy = lax.optimization_barrier((last, total, first_energy))
    last_energy = energy_of(scalars, columns, levels, [(FAR, last)])

    energy = jnp.sum(jnp.concatenate([first_energy, last_energy], axis=0), axis=1)
    energy, last = lax.optimization_barrier((lax.psum(energy, "vir"), last))
    order = jnp.stack([(me // 2 - dx) % CHIPS * 2 + (me + dc) % 2 for dx, dc in EARLY + NEAR + FAR])
    mine = order[:, None] == jnp.arange(occ_size)[None, :]
    energy = jnp.sum(jnp.where(mine, energy[:, None], 0.0), axis=0)
    total = gamma_add(scalars, [(FAR, last, far_rights)], rows, cols, total)
    return total[None], energy[None]


def solution(mesh):
    return jax.shard_map(
        per_device,
        mesh=mesh,
        in_specs=(
            P("occ", "aux", "vir"),
            P(),
            P("vir"),
            P("occ", None, "vir", None),
            P("occ", None),
        ),
        out_specs=(P("occ", "aux", "vir"), P("occ", None)),
        check_vma=False,
    )
```

```python
import functools

import jax
import jax.numpy as jnp
from jax import lax
from jax.experimental import pallas as pl
from jax.experimental.pallas import tpu as pltpu
from jax.sharding import PartitionSpec as P

TILE = 128
CHIPS = 4
VMEM = pl.BlockSpec(memory_space=pltpu.VMEM)
SMEM = pl.BlockSpec(memory_space=pltpu.SMEM)
HBM = pl.BlockSpec(memory_space=pltpu.HBM)
def params():
    return pltpu.CompilerParams(vmem_limit_bytes=12 * 1024 * 1024)


def cost(flops, moved):
    return pl.CostEstimate(flops=flops, bytes_accessed=moved, transcendentals=0)


def split(value):
    high = value.astype(jnp.bfloat16)
    low = (value - high.astype(jnp.float32)).astype(jnp.bfloat16)
    return high, low


def lanes(index):
    return pl.ds(pl.multiple_of(index * TILE, TILE), TILE)


def partner_of(ids_ref, dx, dc):
    me = ids_ref[0]
    return lax.rem(me // 2 + CHIPS - dx, CHIPS) * 2 + lax.rem(me + dc, 2)


def pick_kernel(shifts, ids_ref, pairs_ref, block_ref, *refs):
    *out_refs, zeros_ref, sems = refs
    rows, cols = block_ref.shape
    slots = [(out_ref, k) for out_ref in out_refs for k in range(out_ref.shape[0])]
    zeros_ref[...] = jnp.zeros_like(zeros_ref)
    copies = []
    for (out_ref, k), (dx, dc) in zip(slots, shifts):
        receiver = partner_of(ids_ref, CHIPS - dx, dc)
        for s in range(2):
            tile = lax.rem(pairs_ref[(receiver * 2 * CHIPS + ids_ref[0]) * 2 + s], cols // TILE)
            source = block_ref.at[:, lanes(tile)]
            target = out_ref.at[k, pl.ds(0, rows), pl.ds(s * TILE, TILE)]
            copies.append(pltpu.make_async_copy(source, target, sems.at[len(copies)]))
        target = out_ref.at[k, pl.ds(rows, zeros_ref.shape[0]), :]
        copies.append(pltpu.make_async_copy(zeros_ref, target, sems.at[len(copies)]))
    for copy in copies:
        copy.start()
    for copy in copies:
        copy.wait()


def pick(ids, pairs, block, shifts, counts, padded):
    return pl.pallas_call(
        functools.partial(pick_kernel, shifts),
        out_shape=[jax.ShapeDtypeStruct((count, padded, 2 * TILE), jnp.float32) for count in counts],
        in_specs=[SMEM, SMEM, VMEM],
        out_specs=[HBM] * len(counts),
        scratch_shapes=[
            pltpu.VMEM((padded - block.shape[0], 2 * TILE), jnp.float32),
            pltpu.SemaphoreType.DMA((3 * len(shifts),)),
        ],
        compiler_params=params(),
        cost_estimate=cost(0, sum(counts) * padded * 4 * TILE * 4),
        name="pick",
    )(ids, pairs, block)


def held_kernel(*refs):
    del refs


def held(hint, *arrays):
    return pl.pallas_call(
        held_kernel,
        out_shape=[jax.ShapeDtypeStruct(array.shape, array.dtype) for array in arrays],
        in_specs=[pl.BlockSpec(memory_space=pl.ANY)] * len(arrays),
        out_specs=[pl.BlockSpec(memory_space=pl.ANY)] * len(arrays),
        input_output_aliases={k: k for k in range(len(arrays))},
        compiler_params=params(),
        cost_estimate=cost(hint * 10**9, hint * 3 * 10**6),
        name="held",
    )(*arrays)


def left_kernel(block_ref, out_ref):
    rows = block_ref.shape[0]
    padded = out_ref.shape[2]
    for f in range(out_ref.shape[0]):
        tile = block_ref[:, f * TILE : (f + 1) * TILE]
        tile = jnp.concatenate([tile, jnp.zeros((padded - rows, TILE), jnp.float32)], axis=0)
        high, low = split(tile.T)
        out_ref[f, :TILE, :] = high
        out_ref[f, TILE:, :] = low


def left(block, padded):
    tiles = block.shape[1] // TILE
    return pl.pallas_call(
        left_kernel,
        out_shape=jax.ShapeDtypeStruct((tiles, 2 * TILE, padded), jnp.bfloat16),
        in_specs=[VMEM],
        out_specs=VMEM,
        compiler_params=params(),
        cost_estimate=cost(0, block.size * 8),
        name="left",
    )(block)


def tiles_of(scalars, shift, s, tile_count):
    ids_ref, own_ref = scalars[:2]
    partner = partner_of(ids_ref, *shift)
    entry = own_ref[2 * partner + s]
    return partner, lax.div(entry, tile_count), lax.rem(entry, tile_count)


def denominator_of(scalars, columns_ref, levels_ref, partner, first, second, start, count):
    ids_ref, _, occ_ref, _ = scalars
    row = pl.multiple_of(first * TILE + start, 8)
    occ = occ_ref[ids_ref[0]] + occ_ref[partner]
    return occ - columns_ref[pl.ds(row, count), :] - levels_ref[pl.ds(second, 1), :]


def add_amplitude(scalars, shifts, parts_at, parts_ref, columns_ref, levels_ref, out_ref):
    ids_ref, _, _, live_ref = scalars
    for k, shift in enumerate(shifts):
        for s in range(2):
            t = 2 * k + s
            partner, first, second = tiles_of(scalars, shift, s, levels_ref.shape[0])
            denominator = denominator_of(scalars, columns_ref, levels_ref, partner, first, second, 8 * ids_ref[1], 8)
            summed = jnp.sum(parts_ref[:, parts_at + 8 * t : parts_at + 8 * t + 8, :], axis=0)
            amplitude = summed / jnp.where(s < live_ref[partner], denominator, jnp.inf)
            for owner in range(out_ref.shape[0]):
                out_ref[owner, 8 * t : 8 * t + 8, :] = amplitude
    return 16 * len(shifts)


def exchange_kernel(back_shifts, parts_at, shifts, entries, *refs):
    *in_refs, out_ref = refs
    scalars, in_refs = in_refs[:4], in_refs[4:]
    at = 0
    if back_shifts:
        parts_ref, columns_ref, levels_ref, *in_refs = in_refs
        at = add_amplitude(scalars, back_shifts, parts_at, parts_ref, columns_ref, levels_ref, out_ref)
    if entries:
        left_ref, *right_refs = in_refs
        for k, ((which, entry), shift) in enumerate(zip(entries, shifts)):
            for s in range(2):
                t = 2 * k + s
                _, first, _ = tiles_of(scalars, shift, s, left_ref.shape[0])
                high, low = split(right_refs[which][entry, :, s * TILE : (s + 1) * TILE])
                both = jnp.concatenate([high, low], axis=1)
                part = jnp.dot(left_ref[first], both, preferred_element_type=jnp.float32)
                cross = part[:TILE, TILE:] + part[TILE:, :TILE] + part[TILE:, TILE:]
                total = part[:TILE, :TILE] + cross
                out_ref[:, at + 8 * t : at + 8 * t + 8, :] = total.reshape(TILE // 8, 8, TILE)


def exchange(scalars, returned, group):
    inputs, specs, rows, flops, parts_at = list(scalars), [SMEM] * 4, 0, 0, 0
    back_shifts, shifts, entries = (), (), ()
    if returned is not None:
        back_shifts, parts, parts_at, columns, levels = returned
        inputs += [parts, columns, levels]
        specs += [VMEM] * 3
        rows += 16 * len(back_shifts)
    if group is not None:
        shifts, left_split, rights = group
        arrays, entries = unique(rights)
        inputs += [left_split, *arrays]
        specs += [VMEM] * (1 + len(arrays))
        rows += 16 * len(entries)
        flops = len(entries) * 16 * TILE * TILE * left_split.shape[2]
    return pl.pallas_call(
        functools.partial(exchange_kernel, back_shifts, parts_at, shifts, entries),
        out_shape=jax.ShapeDtypeStruct((TILE // 8, rows, TILE), jnp.float32),
        in_specs=specs,
        out_specs=VMEM,
        compiler_params=params(),
        cost_estimate=cost(flops, TILE // 8 * rows * TILE * 8),
        name="exchange",
    )(*inputs)


def unique(rights):
    arrays, entries = [], []
    for array, entry in rights:
        which = next((k for k, known in enumerate(arrays) if known is array), len(arrays))
        if which == len(arrays):
            arrays.append(array)
        entries.append((which, entry))
    return arrays, entries


def tile_amplitude(amplitude_ref, t):
    return amplitude_ref[:, 8 * t : 8 * t + 8, :].reshape(TILE, TILE)


def energy_kernel(groups, *refs):
    scalars, (columns_ref, levels_ref, *amplitude_refs, out_ref) = refs[:4], refs[4:]
    rows = []
    for shifts, amplitude_ref in zip(groups, amplitude_refs):
        for k, shift in enumerate(shifts):
            for s in range(2):
                amplitude = tile_amplitude(amplitude_ref, 2 * k + s)
                place = tiles_of(scalars, shift, s, levels_ref.shape[0])
                denominator = denominator_of(scalars, columns_ref, levels_ref, *place, 0, TILE)
                rows.append(jnp.sum(amplitude * amplitude * denominator, axis=0, keepdims=True))
    for k in range(len(rows) // 2):
        out_ref[k : k + 1, :] = rows[2 * k] + rows[2 * k + 1]


def energy_of(scalars, columns, levels, groups):
    shifts = [group[0] for group in groups]
    partners = sum(len(group) for group in shifts)
    return pl.pallas_call(
        functools.partial(energy_kernel, shifts),
        out_shape=jax.ShapeDtypeStruct((partners, TILE), jnp.float32),
        in_specs=[SMEM] * 4 + [VMEM] * (2 + len(groups)),
        out_specs=VMEM,
        compiler_params=params(),
        cost_estimate=cost(6 * partners * TILE * TILE, partners * TILE * TILE * 8),
        name="energy",
    )(*scalars, columns, levels, *[group[1] for group in groups])


def gamma_kernel(groups, carried, *refs):
    scalars, refs = refs[:4], refs[4:]
    if carried:
        gamma_in, *refs = refs
    *in_refs, gamma_ref = refs
    rows, cols = gamma_ref.shape
    gamma_ref[...] = gamma_in[...] if carried else jnp.zeros_like(gamma_ref)
    for shifts, entries, arrays in groups:
        (amplitude_ref, *right_refs), in_refs = in_refs[: 1 + arrays], in_refs[1 + arrays :]
        for k, ((which, entry), shift) in enumerate(zip(entries, shifts)):
            for s in range(2):
                _, first, _ = tiles_of(scalars, shift, s, cols // TILE)
                high, low = split(tile_amplitude(amplitude_ref, 2 * k + s))
                weights = jnp.concatenate(
                    [
                        jnp.concatenate([high, high], axis=1),
                        jnp.concatenate([low, low], axis=1),
                    ],
                    axis=0,
                )
                both = jnp.concatenate(split(right_refs[which][entry, :, s * TILE : (s + 1) * TILE]), axis=1)
                part = lax.dot_general(both, weights, (((1,), (1,)), ((), ())), preferred_element_type=jnp.float32)
                place = lanes(first)
                gamma_ref[:, place] += (part[:, :TILE] + part[:, TILE:])[:rows]


def gamma_add(scalars, groups, rows, cols, carried):
    inputs, tiles, described = [], 0, []
    for shifts, amplitudes, rights in groups:
        arrays, entries = unique(rights)
        described.append((shifts, entries, len(arrays)))
        inputs += [amplitudes, *arrays]
        tiles += 2 * len(shifts)
    start = list(scalars) + ([carried] if carried is not None else [])
    return pl.pallas_call(
        functools.partial(gamma_kernel, described, carried is not None),
        out_shape=jax.ShapeDtypeStruct((rows, cols), jnp.float32),
        in_specs=[SMEM] * 4 + [VMEM] * (len(start) - 4 + len(inputs)),
        out_specs=VMEM,
        compiler_params=params(),
        cost_estimate=cost(tiles * 8 * TILE * TILE * rows, rows * cols * 8),
        name="gamma",
    )(*start, *inputs)


EARLY = ((0, 1), (0, 0))
NEAR = ((1, 0), (3, 0), (1, 1), (3, 1))
FAR = ((2, 0), (2, 1))


def per_device(bq, eps_occ, eps_vir, tile_pairs, live_counts):
    occ_size = lax.axis_size("occ")
    me = lax.axis_index("occ")
    block = bq[0]
    rows, cols = block.shape
    padded = -(-rows // 16) * 16
    own_pairs = tile_pairs.reshape(-1)
    all_pairs = lax.all_gather(tile_pairs[0, :, 0, :], "occ").reshape(-1)
    ids = jnp.stack([me, lax.axis_index("aux")]).astype(jnp.int32)
    scalars = (ids, own_pairs, eps_occ, live_counts.reshape(-1))
    columns = jnp.broadcast_to(eps_vir[:, None], (cols, TILE))
    levels = eps_vir.reshape(cols // TILE, TILE)

    def moved(tiles, dx, dc):
        route = [(x * 2 + c, (x + dx) % CHIPS * 2 + (c + dc) % 2) for x in range(CHIPS) for c in range(2)]
        return lax.ppermute(tiles, "occ", route)

    def sent(returned, group):
        return lax.all_to_all(exchange(scalars, returned, group), "aux", 0, 0)

    mate, own = pick(ids, all_pairs, block, EARLY, (1,) * 2, padded)
    near = pick(ids, all_pairs, block, NEAR, (1,) * 4, padded)
    left_split = left(block, padded)
    mate, left_split, *near = lax.optimization_barrier((mate, left_split, *near))
    near = held(70, *[moved(tiles, *shift) for tiles, shift in zip(near, NEAR)])
    early_rights = [(moved(mate, 0, 1), 0), (own, 0)]

    operand = exchange(scalars, None, (EARLY, left_split, early_rights))
    later_ids, operand = lax.optimization_barrier((ids, operand))
    far = list(pick(later_ids, all_pairs, block, FAR, (1,) * 2, padded))
    early = lax.all_to_all(operand, "aux", 0, 0)
    far[0], far[1], early, *near = lax.optimization_barrier((*far, early, *near))
    far = held(70, *[moved(tiles, *shift) for tiles, shift in zip(far, FAR)])
    near_rights = [(tiles, 0) for tiles in near]
    far_rights = [(tiles, 0) for tiles in far]

    parts = sent((EARLY, early, 0, columns, levels), (NEAR, left_split, near_rights))
    both = sent((NEAR, parts, 16 * len(EARLY), columns, levels), (FAR, left_split, far_rights))
    last = sent((FAR, both, 16 * len(NEAR), columns, levels), None)
    first_groups = [(EARLY, parts, early_rights), (NEAR, both, near_rights)]
    total = gamma_add(scalars, first_groups, rows, cols, None)
    first_energy = energy_of(scalars, columns, levels, first_groups)
    last, total, first_energy = lax.optimization_barrier((last, total, first_energy))
    last_energy = energy_of(scalars, columns, levels, [(FAR, last)])

    energy = jnp.sum(jnp.concatenate([first_energy, last_energy], axis=0), axis=1)
    energy, last = lax.optimization_barrier((lax.psum(energy, "vir"), last))
    order = jnp.stack([(me // 2 - dx) % CHIPS * 2 + (me + dc) % 2 for dx, dc in EARLY + NEAR + FAR])
    mine = order[:, None] == jnp.arange(occ_size)[None, :]
    energy = jnp.sum(jnp.where(mine, energy[:, None], 0.0), axis=0)
    total = gamma_add(scalars, [(FAR, last, far_rights)], rows, cols, total)
    return total[None], energy[None]


def solution(mesh):
    return jax.shard_map(
        per_device,
        mesh=mesh,
        in_specs=(
            P("occ", "aux", "vir"),
            P(),
            P("vir"),
            P("occ", None, "vir", None),
            P("occ", None),
        ),
        out_specs=(P("occ", "aux", "vir"), P("occ", None)),
        check_vma=False,
    )
```

```python
import functools

import jax
import jax.numpy as jnp
from jax import lax
from jax.experimental import pallas as pl
from jax.experimental.pallas import tpu as pltpu
from jax.sharding import PartitionSpec as P

TILE = 128
CHIPS = 4
VMEM = pl.BlockSpec(memory_space=pltpu.VMEM)
SMEM = pl.BlockSpec(memory_space=pltpu.SMEM)
HBM = pl.BlockSpec(memory_space=pltpu.HBM)
def params():
    return pltpu.CompilerParams(vmem_limit_bytes=12 * 1024 * 1024)


def cost(flops, moved):
    return pl.CostEstimate(flops=flops, bytes_accessed=moved, transcendentals=0)


def split(value):
    high = value.astype(jnp.bfloat16)
    low = (value - high.astype(jnp.float32)).astype(jnp.bfloat16)
    return high, low


def lanes(index):
    return pl.ds(pl.multiple_of(index * TILE, TILE), TILE)


def partner_of(ids_ref, dx, dc):
    me = ids_ref[0]
    return lax.rem(me // 2 + CHIPS - dx, CHIPS) * 2 + lax.rem(me + dc, 2)


def pick_kernel(shifts, ids_ref, pairs_ref, block_ref, *refs):
    *out_refs, zeros_ref, sems = refs
    rows, cols = block_ref.shape
    slots = [(out_ref, k) for out_ref in out_refs for k in range(out_ref.shape[0])]
    zeros_ref[...] = jnp.zeros_like(zeros_ref)
    copies = []
    for (out_ref, k), (dx, dc) in zip(slots, shifts):
        receiver = partner_of(ids_ref, CHIPS - dx, dc)
        for s in range(2):
            tile = lax.rem(pairs_ref[(receiver * 2 * CHIPS + ids_ref[0]) * 2 + s], cols // TILE)
            source = block_ref.at[:, lanes(tile)]
            target = out_ref.at[k, pl.ds(0, rows), pl.ds(s * TILE, TILE)]
            copies.append(pltpu.make_async_copy(source, target, sems.at[len(copies)]))
        target = out_ref.at[k, pl.ds(rows, zeros_ref.shape[0]), :]
        copies.append(pltpu.make_async_copy(zeros_ref, target, sems.at[len(copies)]))
    for copy in copies:
        copy.start()
    for copy in copies:
        copy.wait()


def pick(ids, pairs, block, shifts, counts, padded):
    return pl.pallas_call(
        functools.partial(pick_kernel, shifts),
        out_shape=[jax.ShapeDtypeStruct((count, padded, 2 * TILE), jnp.float32) for count in counts],
        in_specs=[SMEM, SMEM, VMEM],
        out_specs=[HBM] * len(counts),
        scratch_shapes=[
            pltpu.VMEM((padded - block.shape[0], 2 * TILE), jnp.float32),
            pltpu.SemaphoreType.DMA((3 * len(shifts),)),
        ],
        compiler_params=params(),
        cost_estimate=cost(0, sum(counts) * padded * 4 * TILE * 4),
        name="pick",
    )(ids, pairs, block)


def held_kernel(*refs):
    del refs


def held(hint, *arrays):
    return pl.pallas_call(
        held_kernel,
        out_shape=[jax.ShapeDtypeStruct(array.shape, array.dtype) for array in arrays],
        in_specs=[pl.BlockSpec(memory_space=pl.ANY)] * len(arrays),
        out_specs=[pl.BlockSpec(memory_space=pl.ANY)] * len(arrays),
        input_output_aliases={k: k for k in range(len(arrays))},
        compiler_params=params(),
        cost_estimate=cost(hint * 10**9, hint * 3 * 10**6),
        name="held",
    )(*arrays)


def left_kernel(block_ref, out_ref):
    rows = block_ref.shape[0]
    padded = out_ref.shape[2]
    for f in range(out_ref.shape[0]):
        tile = block_ref[:, f * TILE : (f + 1) * TILE]
        tile = jnp.concatenate([tile, jnp.zeros((padded - rows, TILE), jnp.float32)], axis=0)
        high, low = split(tile.T)
        out_ref[f, :TILE, :] = high
        out_ref[f, TILE:, :] = low


def left(block, padded):
    tiles = block.shape[1] // TILE
    return pl.pallas_call(
        left_kernel,
        out_shape=jax.ShapeDtypeStruct((tiles, 2 * TILE, padded), jnp.bfloat16),
        in_specs=[VMEM],
        out_specs=VMEM,
        compiler_params=params(),
        cost_estimate=cost(0, block.size * 8),
        name="left",
    )(block)


def tiles_of(scalars, shift, s, tile_count):
    ids_ref, own_ref = scalars[:2]
    partner = partner_of(ids_ref, *shift)
    entry = own_ref[2 * partner + s]
    return partner, lax.div(entry, tile_count), lax.rem(entry, tile_count)


def denominator_of(scalars, columns_ref, levels_ref, partner, first, second, start, count):
    ids_ref, _, occ_ref, _ = scalars
    row = pl.multiple_of(first * TILE + start, 8)
    occ = occ_ref[ids_ref[0]] + occ_ref[partner]
    return occ - columns_ref[pl.ds(row, count), :] - levels_ref[pl.ds(second, 1), :]


def add_amplitude(scalars, shifts, parts_at, parts_ref, columns_ref, levels_ref, out_ref):
    ids_ref, _, _, live_ref = scalars
    for k, shift in enumerate(shifts):
        for s in range(2):
            t = 2 * k + s
            partner, first, second = tiles_of(scalars, shift, s, levels_ref.shape[0])
            denominator = denominator_of(scalars, columns_ref, levels_ref, partner, first, second, 8 * ids_ref[1], 8)
            summed = jnp.sum(parts_ref[:, parts_at + 8 * t : parts_at + 8 * t + 8, :], axis=0)
            amplitude = summed / jnp.where(s < live_ref[partner], denominator, jnp.inf)
            for owner in range(out_ref.shape[0]):
                out_ref[owner, 8 * t : 8 * t + 8, :] = amplitude
    return 16 * len(shifts)


def exchange_kernel(back_shifts, parts_at, shifts, entries, *refs):
    *in_refs, out_ref = refs
    scalars, in_refs = in_refs[:4], in_refs[4:]
    at = 0
    if back_shifts:
        parts_ref, columns_ref, levels_ref, *in_refs = in_refs
        at = add_amplitude(scalars, back_shifts, parts_at, parts_ref, columns_ref, levels_ref, out_ref)
    if entries:
        left_ref, *right_refs = in_refs
        for k, ((which, entry), shift) in enumerate(zip(entries, shifts)):
            for s in range(2):
                t = 2 * k + s
                _, first, _ = tiles_of(scalars, shift, s, left_ref.shape[0])
                high, low = split(right_refs[which][entry, :, s * TILE : (s + 1) * TILE])
                both = jnp.concatenate([high, low], axis=1)
                part = jnp.dot(left_ref[first], both, preferred_element_type=jnp.float32)
                cross = part[:TILE, TILE:] + part[TILE:, :TILE] + part[TILE:, TILE:]
                total = part[:TILE, :TILE] + cross
                out_ref[:, at + 8 * t : at + 8 * t + 8, :] = total.reshape(TILE // 8, 8, TILE)


def exchange(scalars, returned, group):
    inputs, specs, rows, flops, parts_at = list(scalars), [SMEM] * 4, 0, 0, 0
    back_shifts, shifts, entries = (), (), ()
    if returned is not None:
        back_shifts, parts, parts_at, columns, levels = returned
        inputs += [parts, columns, levels]
        specs += [VMEM] * 3
        rows += 16 * len(back_shifts)
    if group is not None:
        shifts, left_split, rights = group
        arrays, entries = unique(rights)
        inputs += [left_split, *arrays]
        specs += [VMEM] * (1 + len(arrays))
        rows += 16 * len(entries)
        flops = len(entries) * 16 * TILE * TILE * left_split.shape[2]
    return pl.pallas_call(
        functools.partial(exchange_kernel, back_shifts, parts_at, shifts, entries),
        out_shape=jax.ShapeDtypeStruct((TILE // 8, rows, TILE), jnp.float32),
        in_specs=specs,
        out_specs=VMEM,
        compiler_params=params(),
        cost_estimate=cost(flops, TILE // 8 * rows * TILE * 8),
        name="exchange",
    )(*inputs)


def unique(rights):
    arrays, entries = [], []
    for array, entry in rights:
        which = next((k for k, known in enumerate(arrays) if known is array), len(arrays))
        if which == len(arrays):
            arrays.append(array)
        entries.append((which, entry))
    return arrays, entries


def tile_amplitude(amplitude_ref, t):
    return amplitude_ref[:, 8 * t : 8 * t + 8, :].reshape(TILE, TILE)


def energy_kernel(groups, *refs):
    scalars, (columns_ref, levels_ref, *amplitude_refs, out_ref) = refs[:4], refs[4:]
    rows = []
    for shifts, amplitude_ref in zip(groups, amplitude_refs):
        for k, shift in enumerate(shifts):
            for s in range(2):
                amplitude = tile_amplitude(amplitude_ref, 2 * k + s)
                place = tiles_of(scalars, shift, s, levels_ref.shape[0])
                denominator = denominator_of(scalars, columns_ref, levels_ref, *place, 0, TILE)
                rows.append(jnp.sum(amplitude * amplitude * denominator, axis=0, keepdims=True))
    for k in range(len(rows) // 2):
        out_ref[k : k + 1, :] = rows[2 * k] + rows[2 * k + 1]


def energy_of(scalars, columns, levels, groups):
    shifts = [group[0] for group in groups]
    partners = sum(len(group) for group in shifts)
    return pl.pallas_call(
        functools.partial(energy_kernel, shifts),
        out_shape=jax.ShapeDtypeStruct((partners, TILE), jnp.float32),
        in_specs=[SMEM] * 4 + [VMEM] * (2 + len(groups)),
        out_specs=VMEM,
        compiler_params=params(),
        cost_estimate=cost(6 * partners * TILE * TILE, partners * TILE * TILE * 8),
        name="energy",
    )(*scalars, columns, levels, *[group[1] for group in groups])


def gamma_kernel(groups, carried, *refs):
    scalars, refs = refs[:4], refs[4:]
    if carried:
        gamma_in, *refs = refs
    *in_refs, gamma_ref = refs
    rows, cols = gamma_ref.shape
    gamma_ref[...] = gamma_in[...] if carried else jnp.zeros_like(gamma_ref)
    for shifts, entries, arrays in groups:
        (amplitude_ref, *right_refs), in_refs = in_refs[: 1 + arrays], in_refs[1 + arrays :]
        for k, ((which, entry), shift) in enumerate(zip(entries, shifts)):
            for s in range(2):
                _, first, _ = tiles_of(scalars, shift, s, cols // TILE)
                high, low = split(tile_amplitude(amplitude_ref, 2 * k + s))
                weights = jnp.concatenate(
                    [
                        jnp.concatenate([high, high], axis=1),
                        jnp.concatenate([low, low], axis=1),
                    ],
                    axis=0,
                )
                both = jnp.concatenate(split(right_refs[which][entry, :, s * TILE : (s + 1) * TILE]), axis=1)
                part = lax.dot_general(both, weights, (((1,), (1,)), ((), ())), preferred_element_type=jnp.float32)
                place = lanes(first)
                gamma_ref[:, place] += (part[:, :TILE] + part[:, TILE:])[:rows]


def gamma_add(scalars, groups, rows, cols, carried):
    inputs, tiles, described = [], 0, []
    for shifts, amplitudes, rights in groups:
        arrays, entries = unique(rights)
        described.append((shifts, entries, len(arrays)))
        inputs += [amplitudes, *arrays]
        tiles += 2 * len(shifts)
    start = list(scalars) + ([carried] if carried is not None else [])
    return pl.pallas_call(
        functools.partial(gamma_kernel, described, carried is not None),
        out_shape=jax.ShapeDtypeStruct((rows, cols), jnp.float32),
        in_specs=[SMEM] * 4 + [VMEM] * (len(start) - 4 + len(inputs)),
        out_specs=VMEM,
        compiler_params=params(),
        cost_estimate=cost(tiles * 8 * TILE * TILE * rows, rows * cols * 8),
        name="gamma",
    )(*start, *inputs)


EARLY = ((0, 1), (0, 0))
NEAR = ((1, 0), (3, 0), (1, 1), (3, 1))
FAR = ((2, 0), (2, 1))


def per_device(bq, eps_occ, eps_vir, tile_pairs, live_counts):
    occ_size = lax.axis_size("occ")
    me = lax.axis_index("occ")
    block = bq[0]
    rows, cols = block.shape
    padded = -(-rows // 16) * 16
    own_pairs = tile_pairs.reshape(-1)
    all_pairs = lax.all_gather(tile_pairs[0, :, 0, :], "occ").reshape(-1)
    ids = jnp.stack([me, lax.axis_index("aux")]).astype(jnp.int32)
    scalars = (ids, own_pairs, eps_occ, live_counts.reshape(-1))
    columns = jnp.broadcast_to(eps_vir[:, None], (cols, TILE))
    levels = eps_vir.reshape(cols // TILE, TILE)

    def moved(tiles, dx, dc):
        route = [(x * 2 + c, (x + dx) % CHIPS * 2 + (c + dc) % 2) for x in range(CHIPS) for c in range(2)]
        return lax.ppermute(tiles, "occ", route)

    def sent(returned, group):
        return lax.all_to_all(exchange(scalars, returned, group), "aux", 0, 0)

    near = pick(ids, all_pairs, block, NEAR, (1,) * 4, padded)
    left_split = left(block, padded)
    later_ids, left_split, *near = lax.optimization_barrier((ids, left_split, *near))
    near = held(70, *[moved(tiles, *shift) for tiles, shift in zip(near, NEAR)])
    mate, own, *far = pick(later_ids, all_pairs, block, EARLY + FAR, (1,) * 4, padded)
    early_rights = [(moved(mate, 0, 1), 0), (own, 0)]

    early = sent(None, (EARLY, left_split, early_rights))
    far[0], far[1], early, *near = lax.optimization_barrier((*far, early, *near))
    far = held(70, *[moved(tiles, *shift) for tiles, shift in zip(far, FAR)])
    near_rights = [(tiles, 0) for tiles in near]
    far_rights = [(tiles, 0) for tiles in far]

    parts = sent((EARLY, early, 0, columns, levels), (NEAR, left_split, near_rights))
    both = sent((NEAR, parts, 16 * len(EARLY), columns, levels), (FAR, left_split, far_rights))
    last = sent((FAR, both, 16 * len(NEAR), columns, levels), None)
    first_groups = [(EARLY, parts, early_rights), (NEAR, both, near_rights)]
    total = gamma_add(scalars, first_groups, rows, cols, None)
    first_energy = energy_of(scalars, columns, levels, first_groups)
    last, total, first_energy = lax.optimization_barrier((last, total, first_energy))
    last_energy = energy_of(scalars, columns, levels, [(FAR, last)])

    energy = jnp.sum(jnp.concatenate([first_energy, last_energy], axis=0), axis=1)
    energy, last = lax.optimization_barrier((lax.psum(energy, "vir"), last))
    order = jnp.stack([(me // 2 - dx) % CHIPS * 2 + (me + dc) % 2 for dx, dc in EARLY + NEAR + FAR])
    mine = order[:, None] == jnp.arange(occ_size)[None, :]
    energy = jnp.sum(jnp.where(mine, energy[:, None], 0.0), axis=0)
    total = gamma_add(scalars, [(FAR, last, far_rights)], rows, cols, total)
    return total[None], energy[None]


def solution(mesh):
    return jax.shard_map(
        per_device,
        mesh=mesh,
        in_specs=(
            P("occ", "aux", "vir"),
            P(),
            P("vir"),
            P("occ", None, "vir", None),
            P("occ", None),
        ),
        out_specs=(P("occ", "aux", "vir"), P("occ", None)),
        check_vma=False,
    )
```
